256 devices in a mesh: seq: 2 (over core), dp: 128 (over z, y, x).
Axes of the slice: x: 4, y: 4, z: 8, core: 2. Of those that a mesh axis runs over, the one named last changes fastest.
Arguments:
- hidden: bfloat16 [128, 512, 2560], P('dp', 'seq'), may hold values from -6 to 6
- scan_input: bfloat16 [128, 512, 2560], P('dp', 'seq'), may hold values from -6 to 6
- grad_out: bfloat16 [128, 512, 2560], P('dp', 'seq'), may hold values from -6 to 6
- step_size: float32 [128, 40, 512], P('dp', None, 'seq'), may hold values from 0.5 to 400
- proj_weight: bfloat16 [2560, 256], replicated, may hold values from -0.0068359375 to 0.0068359375
- log_rate: float32 [40], replicated, may hold values from -7.825 to -3.506
- skip_gain: float32 [40], replicated, may hold values from 0.5 to 1.5
- tile_list: int32 [128, 2], P('dp', 'seq'), may hold values from 0 to 1, as said below
Outputs:
- grad_input: bfloat16 [128, 512, 2560], P('dp', 'seq')
- grad_step: float32 [128, 40, 512], P('dp', None, 'seq')
- grad_weight: float32 [2560, 256], P('seq')
- grad_rate: float32 [40], P('seq')
- grad_skip: float32 [40], P('seq')
The draws below stay inside these ranges and needn't reach their ends.
Inputs may be any that keep to these rules, and one draw needn't show every extreme that they name: `tile_list`: for each device, its 1 entries list the local indices of its valid groups in increasing order, then 1 in every unused entry; in every draw some device has the one group valid.
All inputs are finite; a program needn't handle non-finite values.
Results may differ from the reference program's by a relative error of at most 0.003.
Values sent between devices are 32-bit elements; how exact they have to be, the bound alone decides.
No kernel may reach another device: no remote copies, remote signals or barrier semaphores. Data moves between devices by JAX's collectives and lax.ppermute only.
A program may use at most 192 MiB of HBM per device.

```python
import math
import jax
import jax.numpy as jnp
from jax import lax

D = 2560
HEADS = 40
HEAD_DIM = 64
STATE = 128
GROUP = 256
CH_DEV = 1
LEN = 512
GROUPS = 2
SCENES = 128
DI = 2560
N_SEQ = 2


def draw_step_size(key, part):
    key = jax.random.fold_in(key, 11)
    first, second = jax.random.split(key)
    shape = (SCENES, HEADS, LEN)
    base = jnp.exp(jax.random.uniform(first, shape, jnp.float32, math.log(0.5), math.log(2.0)))
    spots = jax.random.randint(second, (SCENES, 2), 0, LEN)
    where_ids = jnp.arange(LEN, dtype=jnp.int32)
    struck = jnp.any(where_ids[None, None, :] == spots[:, :, None], axis=1)
    return jnp.where(struck[:, None, :], 400.0, base).astype(jnp.float32)


def draw_log_rate(key, part):
    key = jax.random.fold_in(key, 23)
    upper_end = math.log(0.03)
    return jax.random.uniform(key, (HEADS,), jnp.float32, math.log(0.0004), upper_end)


def draw_tile_list(key, part):
    key = jax.random.fold_in(key, 37)
    first, second, third = jax.random.split(key, 3)
    valid_bits = jax.random.randint(first, (SCENES, N_SEQ, CH_DEV), 0, 5) < 3
    full_scene = jax.random.randint(second, (), 0, SCENES)
    full_shard = jax.random.randint(third, (), 0, N_SEQ)
    scene_ids = jnp.arange(SCENES, dtype=jnp.int32)[:, None, None]
    shard_ids = jnp.arange(N_SEQ, dtype=jnp.int32)[None, :, None]
    valid_bits = valid_bits | (scene_ids == full_scene) & (shard_ids == full_shard)
    slot_ids = jnp.arange(CH_DEV, dtype=jnp.int32)[None, None, :]
    ranked = jnp.sort(jnp.where(valid_bits, slot_ids, CH_DEV + slot_ids), axis=2)
    listed = jnp.where(ranked < CH_DEV, ranked, CH_DEV)
    return listed.reshape(SCENES, GROUPS).astype(jnp.int32)


def level_of(rng, shape, cuts, smallest, top_value):
    def one(dim, shards_of):
        heights = jax.random.uniform(jax.random.fold_in(jax.random.fold_in(rng, 6), dim), (shards_of,), jnp.float32, smallest / len(cuts), top_value / len(cuts))
        return jnp.repeat(jnp.exp(heights), shape[dim] // shards_of).reshape((-1,) + (1,) * (len(shape) - dim - 1))

    gain = one(*cuts[0])
    for cut in cuts[1:]:
        gain = gain * one(*cut)
    return gain


def noise(own_key, extent, width, limit, cuts=(), kind=jnp.bfloat16):
    loudness = level_of(own_key, extent, cuts, -0.22, 0.18) if cuts else 1.0
    array = jax.random.normal(own_key, extent, jnp.float32) * width * loudness
    return jnp.minimum(jnp.maximum(array, -limit), limit).astype(kind)


def setup_inputs(seed: int = 0) -> dict:
    key_of = jax.random.split(jax.random.key(seed), 9)
    hidden = noise(key_of[0], (SCENES, LEN, D), 1.0, 6.0, ((0, 128), (1, 2)))
    scan_input = noise(key_of[1], (SCENES, LEN, DI), 1.0, 6.0, ((0, 128), (1, 2)))
    grad_out = noise(key_of[2], (SCENES, LEN, DI), 1.0, 6.0, ((0, 128), (1, 2)))
    step_size = draw_step_size(jax.random.fold_in(key_of[8], 71), 0)
    proj_weight = noise(key_of[4], (D, 2 * STATE), (300 * D) ** -0.5, 0.0068359375)
    log_rate = draw_log_rate(jax.random.fold_in(key_of[8], 71), 0)
    skip_gain = jnp.clip(jax.random.uniform(key_of[6], (HEADS,), jnp.float32, 0.5, 1.5), 0.5, 1.5)
    tile_list = draw_tile_list(jax.random.fold_in(key_of[8], 71), 0)
    return {"hidden": hidden, "scan_input": scan_input, "grad_out": grad_out, "step_size": step_size, "proj_weight": proj_weight, "log_rate": log_rate, "skip_gain": skip_gain, "tile_list": tile_list}


exact_mode = lax.Precision.HIGHEST

def group_forward(carry_state, group_values, group_keys, group_query, group_step, decay_rate, gain_vector):
    block_len = group_values.shape[0]
    log_steps = group_step * decay_rate[:, None]
    running = jnp.cumsum(log_steps, axis=1)
    row_index = lax.broadcasted_iota(jnp.int32, (block_len, block_len), 0)
    col_index = lax.broadcasted_iota(jnp.int32, (block_len, block_len), 1)
    causal = row_index >= col_index
    spread = running[:, :, None] - running[:, None, :]
    decays = jnp.exp(jnp.where(causal[None], spread, -jnp.inf))
    scores = jnp.einsum('in,jn->ij', group_query, group_keys, precision=exact_mode)
    mixing = decays * scores[None] * group_step[:, None, :]
    within = jnp.einsum('hij,jhp->ihp', mixing, group_values, precision=exact_mode)
    carried = jnp.einsum('in,hpn->ihp', group_query, carry_state, precision=exact_mode) * jnp.exp(running).T[:, :, None]
    output = within + carried + gain_vector[None, :, None] * group_values
    tail_weight = jnp.exp(running[:, -1:] - running) * group_step
    weighted = group_values * tail_weight.T[:, :, None]
    fresh_state = jnp.einsum('jhp,jn->hpn', weighted, group_keys, precision=exact_mode)
    new_state = jnp.exp(running[:, -1])[:, None, None] * carry_state + fresh_state
    return (new_state, output)

def scene_output(values, projected, masked_step, decay_rate, gain_vector, present):
    values_blocks = values.reshape(GROUPS, GROUP, HEADS, HEAD_DIM)
    key_blocks = projected[:, :STATE].reshape(GROUPS, GROUP, STATE)
    query_blocks = projected[:, STATE:].reshape(GROUPS, GROUP, STATE)
    step_blocks = masked_step.reshape(HEADS, GROUPS, GROUP).transpose(1, 0, 2)

    def advance(carry_state, item):
        group_values, group_keys, group_query, group_step, group_flag = item
        new_state, output = group_forward(carry_state, group_values, group_keys, group_query, group_step, decay_rate, gain_vector)
        return (new_state, output * group_flag)
    start_state = jnp.zeros((HEADS, HEAD_DIM, STATE), jnp.float32)
    _, outputs = lax.scan(advance, start_state, (values_blocks, key_blocks, query_blocks, step_blocks, present))
    return outputs.reshape(LEN, HEADS, HEAD_DIM)

def reference(hidden, scan_input, grad_out, step_size, proj_weight, log_rate, skip_gain, tile_list):
    slot_ids = jnp.arange(CH_DEV, dtype=jnp.int32)
    listed = tile_list.reshape(SCENES, N_SEQ, CH_DEV)
    present_all = jnp.any(listed[:, :, :, None] == slot_ids[None, None, None, :], axis=2)
    present_all = present_all.reshape(SCENES, GROUPS).astype(jnp.float32)

    def per_scene(totals, item):
        activations, inputs_now, upstream, steps_now, present = item
        projected = jnp.dot(activations, proj_weight, preferred_element_type=jnp.float32)
        token_mask = jnp.repeat(present, GROUP)
        upstream_f = upstream.astype(jnp.float32).reshape(LEN, HEADS, HEAD_DIM)

        def scene_loss(values, projected_in, step_in, rate_in, gain_in):
            masked_step = step_in * token_mask[None, :]
            outputs = scene_output(values, projected_in, masked_step, -jnp.exp(rate_in), gain_in, present)
            return jnp.sum(outputs * upstream_f)
        values = inputs_now.astype(jnp.float32).reshape(LEN, HEADS, HEAD_DIM)
        grads = jax.grad(scene_loss, argnums=(0, 1, 2, 3, 4))(values, projected, steps_now, log_rate, skip_gain)
        grad_values, grad_proj, grad_steps, grad_rates, grad_gains = grads
        grad_w = jnp.dot(activations.astype(jnp.float32).T, grad_proj, precision=exact_mode)
        weight_sum, rate_sum, gain_sum = totals
        new_totals = (weight_sum + grad_w, rate_sum + grad_rates, gain_sum + grad_gains)
        return (new_totals, (grad_values.reshape(LEN, DI).astype(jnp.bfloat16), grad_steps))
    start = (jnp.zeros((D, 2 * STATE), jnp.float32), jnp.zeros((HEADS,), jnp.float32), jnp.zeros((HEADS,), jnp.float32))
    totals, per_out = lax.scan(per_scene, start, (hidden, scan_input, grad_out, step_size, present_all))
    grad_input, grad_step = per_out
    return (grad_input, grad_step, totals[0] / SCENES, totals[1] / SCENES, totals[2] / SCENES)
```

```python
import jax
import jax.numpy as jnp
from jax import lax
from jax.experimental import pallas as pl
from jax.experimental.pallas import tpu as pltpu
from jax.sharding import PartitionSpec as P

F32 = jnp.float32
BF16 = jnp.bfloat16
HEADS = 40
WIDTH = 64
STATE = 128
TOK = 256
FEAT = HEADS * WIDTH
SCENES = 128
STEP_HEADS = 8
GROUPS = HEADS // STEP_HEADS
STEP_FEAT = STEP_HEADS * WIDTH
HALF = FEAT // 2
VMEM = 48 * 1024 * 1024

NN = (((1,), (0,)), ((), ()))
NT = (((1,), (1,)), ((), ()))
TN = (((0,), (0,)), ((), ()))


def dot(a, b, dims):
    return lax.dot_general(a, b, dims, preferred_element_type=F32)


def split2(v):
    high = v.astype(BF16)
    return high, (v - high.astype(F32)).astype(BF16)


def split3(v):
    rows = v.shape[0]
    high = v.astype(BF16).astype(F32)
    rest = v - high
    mid = rest.astype(BF16).astype(F32)
    low = rest - mid
    parts = [high, mid, low]
    extra = -3 * rows % 16
    if extra:
        parts.append(jnp.zeros((extra, v.shape[1]), F32))
    return jnp.concatenate(parts, axis=0).astype(BF16)


def dot3(a, b, dims):
    ah, al = split2(a)
    bh, bl = split2(b)
    return dot(ah, bh, dims) + dot(al, bh, dims) + dot(ah, bl, dims)


def head_rows(rows, heads, width):
    row = lax.broadcasted_iota(jnp.int32, (rows, width), 0)
    head = lax.broadcasted_iota(jnp.int32, (rows, width), 1) // WIDTH
    hit = (head == row) | (head == row - heads) | (head == row - 2 * heads)
    return jnp.where(hit & (row < 3 * heads), 1.0, 0.0)


def spread_heads(v, width):
    parts = split3(v)
    return dot(parts, head_rows(parts.shape[0], v.shape[0], width).astype(BF16), TN)


def sum_parts(v, heads):
    return v[:heads] + v[heads : 2 * heads] + v[2 * heads : 3 * heads]


def state_kernel(
    tile_ref, hidden_hbm, weight_hbm, x_hbm, g_hbm, step_ref, rate_ref,
    proj_ref, run_ref, cols_ref, scale_ref, high_ref, low_ref, send_ref,
    hidden, weight, values, sems,
):
    role = lax.axis_index("seq")
    copies = []
    for c in range(GROUPS):
        part = pl.ds(c * STEP_FEAT, STEP_FEAT)
        copies.append(pltpu.make_async_copy(hidden_hbm.at[:, part], hidden.at[:, part], sems.at[c]))
        copies.append(pltpu.make_async_copy(weight_hbm.at[part], weight.at[part], sems.at[GROUPS + c]))
    for copy in copies:
        copy.start()
    take_x = pltpu.make_async_copy(x_hbm, values, sems.at[2 * GROUPS])
    take_g = pltpu.make_async_copy(g_hbm, values, sems.at[2 * GROUPS])

    @pl.when(role == 0)
    def _():
        take_x.start()

    @pl.when(role != 0)
    def _():
        take_g.start()

    present = jnp.where(tile_ref[0, 0] == 0, 1.0, 0.0).astype(F32)
    step = step_ref[...]
    rate = -jnp.exp(rate_ref[...])
    logs = step * present * rate
    row = lax.broadcasted_iota(jnp.int32, (TOK, TOK), 0)
    col = lax.broadcasted_iota(jnp.int32, (TOK, TOK), 1)
    upto = jnp.where(row <= col, 1.0, 0.0).astype(BF16)
    run = sum_parts(dot(split3(logs), upto, NN), HEADS)
    run_ref[...] = run
    less = run - jnp.log(step)
    turned = jnp.concatenate([less, jnp.zeros((STATE - HEADS, TOK), F32)], axis=0).T
    for k in range(GROUPS):
        cols_ref[k] = turned[:, k * STEP_HEADS : (k + 1) * STEP_HEADS]
    tail = step * jnp.exp(run[:, TOK - 1 :] - run)
    scale = jnp.where(role == 0, tail, jnp.exp(run)) * present
    scale_ref[...] = scale

    proj = jnp.zeros((TOK, 2 * STATE), F32)
    for c in range(GROUPS):
        copies[2 * c].wait()
        copies[2 * c + 1].wait()
        part = slice(c * STEP_FEAT, (c + 1) * STEP_FEAT)
        proj = proj + dot(hidden[:, part], weight[part, :], NN)
    proj_ref[...] = proj
    mine = jnp.where(role == 0, proj[:, :STATE], proj[:, STATE:])
    mine_high, mine_low = split2(mine)
    take_x.wait()
    parts = split3(scale)
    for c in range(GROUPS):
        part = slice(c * STEP_FEAT, (c + 1) * STEP_FEAT)
        r = lax.broadcasted_iota(jnp.int32, (parts.shape[0], STEP_FEAT), 0)
        h = lax.broadcasted_iota(jnp.int32, (parts.shape[0], STEP_FEAT), 1) // WIDTH + c * STEP_HEADS
        hit = (h == r) | (h == r - HEADS) | (h == r - 2 * HEADS)
        pick = jnp.where(hit, 1.0, 0.0).astype(BF16)
        scaled = dot(parts, pick, TN) * values[:, part].astype(F32)
        high, low = split2(scaled)
        high_ref[:, part] = high
        low_ref[:, part] = low
        send_ref[:, part] = dot(mine_high, high, TN) + dot(mine_low, high, TN) + dot(mine_high, low, TN)


def state_call(tile, hidden, weight, x, g, step, log_rate):
    vm = pl.BlockSpec(memory_space=pltpu.VMEM)
    hbm = pl.BlockSpec(memory_space=pl.ANY)
    return pl.pallas_call(
        state_kernel,
        name="state_to_send",
        out_shape=(
            jax.ShapeDtypeStruct((TOK, 2 * STATE), F32),
            jax.ShapeDtypeStruct((HEADS, TOK), F32),
            jax.ShapeDtypeStruct((GROUPS, TOK, STEP_HEADS), F32),
            jax.ShapeDtypeStruct((HEADS, TOK), F32),
            jax.ShapeDtypeStruct((TOK, FEAT), BF16),
            jax.ShapeDtypeStruct((TOK, FEAT), BF16),
            jax.ShapeDtypeStruct((STATE, FEAT), F32),
        ),
        in_specs=[pl.BlockSpec(memory_space=pltpu.SMEM), hbm, hbm, hbm, hbm, vm, vm],
        out_specs=(vm,) * 7,
        scratch_shapes=[
            pltpu.VMEM((TOK, FEAT), BF16),
            pltpu.VMEM((FEAT, 2 * STATE), BF16),
            pltpu.VMEM((TOK, FEAT), BF16),
            pltpu.SemaphoreType.DMA((2 * GROUPS + 1,)),
        ],
        compiler_params=pltpu.CompilerParams(vmem_limit_bytes=VMEM),
        cost_estimate=pl.CostEstimate(flops=1_000_000_000, bytes_accessed=8_000_000, transcendentals=20_000),
    )(tile, hidden, weight, x, g, step, log_rate)


def causal_bias():
    row = lax.broadcasted_iota(jnp.int32, (STATE, STATE), 0)
    col = lax.broadcasted_iota(jnp.int32, (STATE, STATE), 1)
    return jnp.where(col >= row, 0.0, -1e30).astype(F32)


def own_half(v, which):
    lane = lax.broadcasted_iota(jnp.int32, v.shape, 1)
    keep = (lane < WIDTH) if which == 0 else (lane >= WIDTH)
    return jnp.where(keep, v, jnp.zeros_like(v))


def decays(run_row, less_col, bias):
    d = run_row - less_col
    first = jnp.exp(jnp.concatenate([d[:STATE, :STATE] + bias, d[:STATE, STATE:]], axis=1))
    second = jnp.exp(d[STATE:, STATE:] + bias)
    return first, second


def pair_kernel(x_ref, g_ref, run_ref, cols_ref, out_ref):
    bias = causal_bias()
    first = jnp.zeros((STATE, TOK), F32)
    second = jnp.zeros((STATE, STATE), F32)
    for r in range(STEP_HEADS):
        lanes = slice(r // 2 * 128, r // 2 * 128 + 128)
        x = x_ref[:, lanes]
        g = own_half(g_ref[:, lanes], r % 2)
        d1, d2 = decays(run_ref[r : r + 1, :], cols_ref[0][:, r : r + 1], bias)
        first = first + d1 * dot(x[:STATE], g, NT)
        second = second + d2 * dot(x[STATE:], g[STATE:], NT)

    @pl.when(pl.program_id(0) == 0)
    def _():
        out_ref[...] = jnp.zeros_like(out_ref)

    out_ref[:STATE, :] += first
    out_ref[STATE:, STATE:] += second


def pair_call(x, g, run, cols):
    return pl.pallas_call(
        pair_kernel,
        name="score_gradient",
        grid=(GROUPS,),
        out_shape=jax.ShapeDtypeStruct((TOK, TOK), F32),
        in_specs=[
            pl.BlockSpec((TOK, STEP_FEAT), lambda k: (0, k)),
            pl.BlockSpec((TOK, STEP_FEAT), lambda k: (0, k)),
            pl.BlockSpec((STEP_HEADS, TOK), lambda k: (k, 0)),
            pl.BlockSpec((1, TOK, STEP_HEADS), lambda k: (k, 0, 0)),
        ],
        out_specs=pl.BlockSpec((TOK, TOK), lambda k: (0, 0)),
        compiler_params=pltpu.CompilerParams(vmem_limit_bytes=VMEM),
        cost_estimate=pl.CostEstimate(flops=1_500_000_000, bytes_accessed=3_000_000, transcendentals=2_600_000),
    )(x, g, run, cols)


def weight_kernel(
    tile_ref, pair_ref, proj_ref, high_ref, low_ref, state_ref, hidden_ref, keep_ref, send_ref
):
    role = lax.axis_index("seq")
    present = jnp.where(tile_ref[0, 0] == 0, 1.0, 0.0).astype(F32)
    pair = pair_ref[...] * present
    proj = proj_ref[...]
    keys = dot3(pair, proj[:, STATE:], NN)
    query = dot3(pair, proj[:, :STATE], TN)
    both = jnp.concatenate(split2(state_ref[...]), axis=0)
    high = dot(high_ref[...], both, NT)
    across = high[:, :STATE] + high[:, STATE:] + dot(low_ref[...], both[:STATE], NT)
    keys = keys + jnp.where(role == 0, across, 0.0)
    query = query + jnp.where(role == 0, 0.0, across)
    grad = jnp.concatenate([keys, query], axis=1) * (1.0 / SCENES)
    terms = jnp.concatenate(split2(grad), axis=1)
    chunk = 256
    for out_ref, base in ((send_ref, (1 - role) * HALF), (keep_ref, role * HALF)):
        for c in range(HALF // chunk):
            lanes = pl.ds(pl.multiple_of(base + c * chunk, 128), chunk)
            got = dot(hidden_ref[:, lanes], terms, TN)
            out_ref[c * chunk : (c + 1) * chunk, :] = got[:, : 2 * STATE] + got[:, 2 * STATE :]


def weight_call(tile, pair, proj, high, low, state, hidden):
    vm = pl.BlockSpec(memory_space=pltpu.VMEM)
    return pl.pallas_call(
        weight_kernel,
        name="weight_gradient",
        out_shape=(
            jax.ShapeDtypeStruct((HALF, 2 * STATE), F32),
            jax.ShapeDtypeStruct((HALF, 2 * STATE), F32),
        ),
        in_specs=[pl.BlockSpec(memory_space=pltpu.SMEM)] + [vm] * 6,
        out_specs=(vm, vm),
        compiler_params=pltpu.CompilerParams(vmem_limit_bytes=VMEM),
        cost_estimate=pl.CostEstimate(flops=1_500_000_000, bytes_accessed=8_000_000, transcendentals=0),
    )(tile, pair, proj, high, low, state, hidden)


def input_kernel(
    tile_ref, x_ref, g_ref, run_ref, cols_ref, scale_ref, step_ref, rate_ref, gain_ref, state_ref, proj_ref,
    dx_ref, dstep_ref, small_ref,
    scores, rows,
):
    role = lax.axis_index("seq")
    first_role = jnp.where(role == 0, 1.0, 0.0).astype(F32)
    present = jnp.where(tile_ref[0, 0] == 0, 1.0, 0.0).astype(F32)
    k = pl.program_id(0)

    @pl.when(k == 0)
    def _():
        small_ref[...] = jnp.zeros_like(small_ref)
        scores[...] = dot3(proj_ref[:, :STATE], proj_ref[:, STATE:], NT) * present

    bias = causal_bias()
    state = state_ref[...]
    mine = jnp.where(role == 0, proj_ref[:, :STATE], proj_ref[:, STATE:])
    carried = spread_heads(scale_ref[...], STEP_FEAT) * dot3(mine, state, NN)
    select = head_rows(STEP_HEADS, STEP_HEADS, STEP_FEAT)
    gain_row = jnp.sum(select * gain_ref[...], axis=0, keepdims=True) * present
    x_all = x_ref[...].astype(F32)
    g_all = g_ref[...].astype(F32)
    within = []
    for q in range(STEP_HEADS // 2):
        lanes = slice(q * 128, q * 128 + 128)
        x = x_ref[:, lanes]
        upper = jnp.zeros((STATE, 128), F32)
        lower = jnp.zeros((STATE, 128), F32)
        for half in range(2):
            r = 2 * q + half
            g = own_half(g_ref[:, lanes], half)
            d1, d2 = decays(run_ref[r : r + 1, :], cols_ref[0][:, r : r + 1], bias)
            m1 = d1 * scores[:STATE, :]
            m2 = d2 * scores[STATE:, STATE:]
            f1 = jnp.sum(m1 * dot(x[:STATE], g, NT), axis=0, keepdims=True)
            f2 = jnp.sum(m2 * dot(x[STATE:], g[STATE:], NT), axis=0, keepdims=True)
            rows[r : r + 1, :STATE] = f1[:, :STATE]
            rows[r : r + 1, STATE:] = f1[:, STATE:] + f2
            h1, l1 = split2(m1)
            h2, l2 = split2(m2)
            upper = upper + dot(h1, g, NN) + dot(l1, g, NN)
            lower = lower + dot(h2, g[STATE:], NN) + dot(l2, g[STATE:], NN)
        within.append(jnp.concatenate([upper, lower], axis=0))
    total = jnp.concatenate(within, axis=1) + first_role * carried
    dx_ref[...] = (total + gain_row * g_all).astype(BF16)

    own = jnp.where(role == 0, x_all, g_all)
    pick = jnp.concatenate([select, jnp.zeros_like(select)], axis=0).astype(BF16)
    by_x_high, by_x_low = split2(x_all * total)
    by_x = (dot(pick, by_x_high, NT) + dot(pick, by_x_low, NT))[:STEP_HEADS]
    by_own_high, by_own_low = split2(own * carried)
    by_own = (dot(pick, by_own_high, NT) + dot(pick, by_own_low, NT))[:STEP_HEADS]
    slope = rows[...] - by_x + (1.0 - first_role) * by_own
    row = lax.broadcasted_iota(jnp.int32, (TOK, TOK), 0)
    col = lax.broadcasted_iota(jnp.int32, (TOK, TOK), 1)
    after = jnp.where(row >= col, 1.0, 0.0).astype(BF16)
    logs = sum_parts(dot(split3(slope), after, NN), STEP_HEADS)
    logs = logs + first_role * jnp.sum(by_own, axis=1, keepdims=True)
    step = step_ref[...]
    rate = -jnp.exp(rate_ref[...])
    dstep_ref[...] = by_x / step + rate * logs
    d_rate = rate * present * jnp.sum(step * logs, axis=1, keepdims=True)
    gx = jnp.sum(g_all * x_all, axis=0, keepdims=True) * present
    d_gain = jnp.sum(select * gx, axis=1, keepdims=True)
    r8 = lax.broadcasted_iota(jnp.int32, (8, 128), 0)
    lane = lax.broadcasted_iota(jnp.int32, (8, 128), 1)
    spot = lane == r8 + k * STEP_HEADS
    small_ref[:, :128] += jnp.where(spot, d_rate * (1.0 / SCENES), 0.0)
    small_ref[:, 128:] += jnp.where(spot, d_gain * (1.0 / SCENES), 0.0)


def input_call(tile, x, g, run, cols, scale, step, log_rate, gain, state, proj):
    feat = pl.BlockSpec((TOK, STEP_FEAT), lambda k: (0, k))
    head = pl.BlockSpec((STEP_HEADS, TOK), lambda k: (k, 0))
    one = pl.BlockSpec((STEP_HEADS, 1), lambda k: (k, 0))
    return pl.pallas_call(
        input_kernel,
        name="input_gradient",
        grid=(GROUPS,),
        out_shape=(
            jax.ShapeDtypeStruct((TOK, FEAT), BF16),
            jax.ShapeDtypeStruct((HEADS, TOK), F32),
            jax.ShapeDtypeStruct((8, 256), F32),
        ),
        in_specs=[
            pl.BlockSpec(memory_space=pltpu.SMEM),
            feat,
            feat,
            head,
            pl.BlockSpec((1, TOK, STEP_HEADS), lambda k: (k, 0, 0)),
            head,
            head,
            one,
            one,
            pl.BlockSpec((STATE, STEP_FEAT), lambda k: (0, k)),
            pl.BlockSpec((TOK, 2 * STATE), lambda k: (0, 0)),
        ],
        out_specs=(feat, head, pl.BlockSpec((8, 256), lambda k: (0, 0))),
        scratch_shapes=[pltpu.VMEM((TOK, TOK), F32), pltpu.VMEM((STEP_HEADS, TOK), F32)],
        compiler_params=pltpu.CompilerParams(vmem_limit_bytes=VMEM),
        cost_estimate=pl.CostEstimate(flops=6_000_000_000, bytes_accessed=8_000_000, transcendentals=2_600_000),
    )(tile, x, g, run, cols, scale, step, log_rate, gain, state, proj)


SIZES = {"z": 8, "y": 4, "x": 4}
STRIDE = {"z": 16, "y": 4, "x": 1}


def moved(axis, new):
    n, s = SIZES[axis], STRIDE[axis]
    pairs = []
    for i in range(SCENES):
        c = i // s % n
        pairs.append((i, i + (new(c) - c) * s))
    return pairs


def shift(v, axis, k):
    return lax.ppermute(v, "dp", moved(axis, lambda c: (c + k) % SIZES[axis]))


def scatter_sum(v, axis, extra=None):
    n = SIZES[axis]
    r = v.shape[0] // n
    me = lax.axis_index("dp") // STRIDE[axis] % n
    total = lax.dynamic_slice_in_dim(v, me * r, r, 0)
    if extra is not None:
        total = jnp.concatenate([total, extra], axis=0)
    for k in range(1, n):
        piece = lax.dynamic_slice_in_dim(v, lax.rem(me + k, n) * r, r, 0)
        if extra is not None:
            piece = jnp.concatenate([piece, extra], axis=0)
        total = total + shift(piece, axis, k)
    return total


def gather(v, axis):
    n = SIZES[axis]
    me = lax.axis_index("dp") // STRIDE[axis] % n
    return me, [v] + [shift(v, axis, k) for k in range(1, n)]


def laid(me, pieces, r):
    n = len(pieces)
    out = jnp.zeros((n * r, pieces[0].shape[1]), F32)
    for k, piece in enumerate(pieces):
        out = lax.dynamic_update_slice_in_dim(out, piece[:r], lax.rem(me + n - k, n) * r, 0)
    return out


def swap(v):
    return lax.ppermute(v, "seq", [(0, 1), (1, 0)])


def shards(hidden, scan_input, grad_out, step_size, proj_weight, log_rate, skip_gain, tile_list):
    role = lax.axis_index("seq")
    hid, x, g, step = hidden[0], scan_input[0], grad_out[0], step_size[0]
    rate_col = log_rate[:, None]
    gain_col = skip_gain[:, None]
    proj, run, cols, scale, high, low, send = state_call(tile_list, hid, proj_weight, x, g, step, rate_col)
    state = swap(send)
    pair = pair_call(x, g, run, cols)
    keep, give = weight_call(tile_list, pair, proj, high, low, state, hid)
    half = keep + swap(give)
    dx, dstep, small = input_call(
        tile_list, x, g, run, cols, scale, step, rate_col, gain_col, state, proj
    )
    part = scatter_sum(half, "x")
    small = small + swap(small)
    part = scatter_sum(part, "y", small)
    for d in (1, 2, 4):
        part = part + lax.ppermute(part, "dp", moved("z", lambda c, d=d: c ^ d))
    rows = HALF // 16
    me, pieces = gather(part[:rows], "y")
    wide = jnp.concatenate([laid(me, pieces, rows), part[rows:]], axis=0)
    me, pieces = gather(wide, "x")
    grad_weight = laid(me, pieces, rows * 4)
    small = sum(piece[rows * 4 :] for piece in pieces)
    small = jnp.sum(small, axis=0)
    share = HEADS // 2
    d_rate = lax.dynamic_slice_in_dim(small[:HEADS], role * share, share, 0)
    d_gain = lax.dynamic_slice_in_dim(small[128 : 128 + HEADS], role * share, share, 0)
    return dx[None], dstep[None], grad_weight, d_rate, d_gain


def solution(mesh):
    in_specs = (
        P("dp", "seq", None),
        P("dp", "seq", None),
        P("dp", "seq", None),
        P("dp", None, "seq"),
        P(),
        P(),
        P(),
        P("dp", "seq"),
    )
    out_specs = (P("dp", "seq", None), P("dp", None, "seq"), P("seq", None), P("seq"), P("seq"))
    return jax.shard_map(shards, mesh=mesh, in_specs=in_specs, out_specs=out_specs, check_vma=False)
```

```python
import jax
import jax.numpy as jnp
from jax import lax
from jax.experimental import pallas as pl
from jax.experimental.pallas import tpu as pltpu
from jax.sharding import PartitionSpec as P

F32 = jnp.float32
BF16 = jnp.bfloat16
HEADS = 40
WIDTH = 64
STATE = 128
TOK = 256
FEAT = HEADS * WIDTH
SCENES = 128
STEP_HEADS = 8
GROUPS = HEADS // STEP_HEADS
STEP_FEAT = STEP_HEADS * WIDTH
HALF = FEAT // 2
MIB = 1024 * 1024
RING = 4
PIECE = HALF // RING
PLANE = RING * RING
ROWS = HALF // PLANE

NN = (((1,), (0,)), ((), ()))
NT = (((1,), (1,)), ((), ()))
TN = (((0,), (0,)), ((), ()))


def dot(a, b, dims):
    return lax.dot_general(a, b, dims, preferred_element_type=F32)


def split2(v):
    high = v.astype(BF16)
    return high, (v - high.astype(F32)).astype(BF16)


def split3(v):
    rows = v.shape[0]
    high = v.astype(BF16).astype(F32)
    rest = v - high
    mid = rest.astype(BF16).astype(F32)
    low = rest - mid
    parts = [high, mid, low]
    extra = -3 * rows % 16
    if extra:
        parts.append(jnp.zeros((extra, v.shape[1]), F32))
    return jnp.concatenate(parts, axis=0)


def dot3(a, b, dims):
    ah, al = split2(a)
    bh, bl = split2(b)
    return dot(ah, bh, dims) + dot(al, bh, dims) + dot(ah, bl, dims)


def head_rows(rows, heads, width):
    row = lax.broadcasted_iota(jnp.int32, (rows, width), 0)
    head = lax.broadcasted_iota(jnp.int32, (rows, width), 1) // WIDTH
    hit = (head == row) | (head == row - heads) | (head == row - 2 * heads)
    return jnp.where(hit & (row < 3 * heads), 1.0, 0.0)


def spread_heads(v, width):
    parts = split3(v).astype(BF16)
    return dot(parts, head_rows(parts.shape[0], v.shape[0], width).astype(BF16), TN)


def turn_column(row):
    same = lax.broadcasted_iota(jnp.int32, (HEADS, HEADS), 0) == lax.broadcasted_iota(jnp.int32, (HEADS, HEADS), 1)
    return jnp.sum(jnp.where(same, row, 0.0), axis=1, keepdims=True)


def sum_parts(v, heads):
    return v[:heads] + v[heads : 2 * heads] + v[2 * heads : 3 * heads]


def state_kernel(
    tile_ref, hidden_hbm, weight_hbm, x_hbm, g_hbm, step_hbm, rate_ref,
    proj_ref, run_ref, cols_ref, scale_ref, rates_ref, high_ref, low_ref, send_ref, wide_ref,
    hidden, weight, values, step_vm, sems,
):
    role = lax.axis_index("seq")
    take_step = pltpu.make_async_copy(step_hbm, step_vm, sems.at[2 * GROUPS + 1])
    take_step.start()
    copies = []
    for c in range(GROUPS):
        part = pl.ds(c * STEP_FEAT, STEP_FEAT)
        copies.append(pltpu.make_async_copy(hidden_hbm.at[:, part], hidden.at[:, part], sems.at[c]))
        copies.append(pltpu.make_async_copy(weight_hbm.at[part], weight.at[part], sems.at[GROUPS + c]))
    for copy in copies:
        copy.start()
    take_x = pltpu.make_async_copy(x_hbm, values, sems.at[2 * GROUPS])
    take_g = pltpu.make_async_copy(g_hbm, values, sems.at[2 * GROUPS])

    @pl.when(role == 0)
    def _():
        take_x.start()

    @pl.when(role != 0)
    def _():
        take_g.start()

    present = jnp.where(tile_ref[0, 0] == 0, 1.0, 0.0).astype(F32)
    take_step.wait()
    step = step_vm[...]
    rate = -jnp.exp(turn_column(rate_ref[...]))
    rates_ref[...] = jnp.broadcast_to(rate, (HEADS, 128))
    logs = step * present * rate
    row = lax.broadcasted_iota(jnp.int32, (TOK, TOK), 0)
    col = lax.broadcasted_iota(jnp.int32, (TOK, TOK), 1)
    upto = jnp.where(row <= col, 1.0, 0.0).astype(BF16)
    run = sum_parts(dot(split3(logs).astype(BF16), upto, NN), HEADS)
    run_ref[...] = run
    less = run - jnp.log(step)
    turned = jnp.concatenate([less, jnp.zeros((STATE - HEADS, TOK), F32)], axis=0).T
    for k in range(GROUPS):
        cols_ref[k] = turned[:, k * STEP_HEADS : (k + 1) * STEP_HEADS]
    tail = step * jnp.exp(run[:, TOK - 1 :] - run)
    scale = jnp.where(role == 0, tail, jnp.exp(run)) * present
    scale_ref[...] = scale

    proj = jnp.zeros((TOK, 2 * STATE), F32)
    for c in range(GROUPS):
        copies[2 * c].wait()
        copies[2 * c + 1].wait()
        part = slice(c * STEP_FEAT, (c + 1) * STEP_FEAT)
        proj = proj + dot(hidden[:, part], weight[part, :], NN)
    proj_ref[...] = proj
    mine = jnp.where(role == 0, proj[:, :STATE], proj[:, STATE:])
    mine_high, mine_low = split2(mine)
    take_x.wait()
    parts = split3(scale).astype(BF16)
    for c in range(GROUPS):
        part = slice(c * STEP_FEAT, (c + 1) * STEP_FEAT)
        r = lax.broadcasted_iota(jnp.int32, (parts.shape[0], STEP_FEAT), 0)
        h = lax.broadcasted_iota(jnp.int32, (parts.shape[0], STEP_FEAT), 1) // WIDTH + c * STEP_HEADS
        hit = (h == r) | (h == r - HEADS) | (h == r - 2 * HEADS)
        pick = jnp.where(hit, 1.0, 0.0).astype(BF16)
        scaled = dot(parts, pick, TN) * values[:, part].astype(F32)
        high, low = split2(scaled)
        high_ref[:, part] = high
        low_ref[:, part] = low
        send_ref[:, part] = dot(mine_high, high, TN) + dot(mine_low, high, TN) + dot(mine_high, low, TN)
    for c in range(GROUPS):
        lanes = pl.ds(pl.multiple_of((1 - role) * HALF + c * 256, 128), 256)
        wide_ref[:, c * 256 : (c + 1) * 256] = hidden[:, lanes].astype(F32)


def state_call(tile, hidden, weight, x, g, step, log_rate):
    sm = pl.BlockSpec(memory_space=pltpu.SMEM)
    vm = pl.BlockSpec(memory_space=pltpu.VMEM)
    hbm = pl.BlockSpec(memory_space=pltpu.HBM)
    return pl.pallas_call(
        state_kernel,
        name="state_to_send",
        out_shape=(
            jax.ShapeDtypeStruct((TOK, 2 * STATE), F32),
            jax.ShapeDtypeStruct((HEADS, TOK), F32),
            jax.ShapeDtypeStruct((GROUPS, TOK, STEP_HEADS), F32),
            jax.ShapeDtypeStruct((HEADS, TOK), F32),
            jax.ShapeDtypeStruct((HEADS, 128), F32),
            jax.ShapeDtypeStruct((TOK, FEAT), BF16),
            jax.ShapeDtypeStruct((TOK, FEAT), BF16),
            jax.ShapeDtypeStruct((STATE, FEAT), F32),
            jax.ShapeDtypeStruct((TOK, HALF), F32),
        ),
        in_specs=[sm] + [hbm] * 5 + [vm],
        out_specs=(vm,) * 9,
        scratch_shapes=[
            pltpu.VMEM((TOK, FEAT), BF16),
            pltpu.VMEM((FEAT, 2 * STATE), BF16),
            pltpu.VMEM((TOK, FEAT), BF16),
            pltpu.VMEM((HEADS, TOK), F32),
            pltpu.SemaphoreType.DMA((2 * GROUPS + 2,)),
        ],
        compiler_params=pltpu.CompilerParams(vmem_limit_bytes=48 * MIB),
        cost_estimate=pl.CostEstimate(flops=1_000_000_000, bytes_accessed=8_000_000, transcendentals=20_000),
    )(tile, hidden, weight, x, g, step, log_rate)


def causal_bias():
    row = lax.broadcasted_iota(jnp.int32, (STATE, STATE), 0)
    col = lax.broadcasted_iota(jnp.int32, (STATE, STATE), 1)
    return jnp.where(col >= row, 0.0, -1e30).astype(F32)


def own_half(v, which):
    lane = lax.broadcasted_iota(jnp.int32, v.shape, 1)
    keep = (lane < WIDTH) if which == 0 else (lane >= WIDTH)
    return jnp.where(keep, v, jnp.zeros_like(v))


def decays(run_row, less_col, bias):
    d = run_row - less_col
    first = jnp.exp(jnp.concatenate([d[:STATE, :STATE] + bias, d[:STATE, STATE:]], axis=1))
    second = jnp.exp(d[STATE:, STATE:] + bias)
    return first, second


def pair_kernel(x_ref, g_ref, run_ref, cols_ref, out_ref):
    bias = causal_bias()
    first = jnp.zeros((STATE, TOK), F32)
    second = jnp.zeros((STATE, STATE), F32)
    for q in range(STEP_HEADS // 2):
        lanes = slice(q * 128, q * 128 + 128)
        x, g = x_ref[:, lanes], g_ref[:, lanes]
        w = dot(jnp.concatenate([own_half(x, 0), own_half(x, 1)], axis=0), g, NT)
        for half in range(2):
            r = 2 * q + half
            d1, d2 = decays(run_ref[r : r + 1, :], cols_ref[0][:, r : r + 1], bias)
            first = first + d1 * w[half * TOK : half * TOK + STATE]
            second = second + d2 * w[half * TOK + STATE : half * TOK + TOK, STATE:]

    @pl.when(pl.program_id(0) == 0)
    def _():
        out_ref[...] = jnp.zeros_like(out_ref)

    out_ref[:STATE, :] += first
    out_ref[STATE:, STATE:] += second


def pair_call(x, g, run, cols):
    return pl.pallas_call(
        pair_kernel,
        name="score_gradient",
        grid=(GROUPS,),
        out_shape=jax.ShapeDtypeStruct((TOK, TOK), F32),
        in_specs=[
            pl.BlockSpec((TOK, STEP_FEAT), lambda k: (0, k)),
            pl.BlockSpec((TOK, STEP_FEAT), lambda k: (0, k)),
            pl.BlockSpec((STEP_HEADS, TOK), lambda k: (k, 0)),
            pl.BlockSpec((1, TOK, STEP_HEADS), lambda k: (k, 0, 0)),
        ],
        out_specs=pl.BlockSpec((TOK, TOK), lambda k: (0, 0)),
        compiler_params=pltpu.CompilerParams(vmem_limit_bytes=16 * MIB),
        cost_estimate=pl.CostEstimate(flops=1_500_000_000, bytes_accessed=3_000_000, transcendentals=2_600_000),
    )(x, g, run, cols)


def proj_kernel(tile_ref, pair_ref, proj_ref, high_ref, low_ref, state_ref, grad_ref):
    role = lax.axis_index("seq")
    present = jnp.where(tile_ref[0, 0] == 0, 1.0, 0.0).astype(F32)
    pair = pair_ref[...] * present
    proj = proj_ref[...]
    keys = dot3(pair, proj[:, STATE:], NN)
    query = dot3(pair, proj[:, :STATE], TN)
    both = jnp.concatenate(split2(state_ref[...]), axis=0)
    high = dot(high_ref[...], both, NT)
    across = high[:, :STATE] + high[:, STATE:] + dot(low_ref[...], both[:STATE], NT)
    keys = keys + jnp.where(role == 0, across, 0.0)
    query = query + jnp.where(role == 0, 0.0, across)
    grad_ref[...] = jnp.concatenate([keys, query], axis=1) * (1.0 / SCENES)


def proj_call(tile, pair, proj, high, low, state):
    vm = pl.BlockSpec(memory_space=pltpu.VMEM)
    return pl.pallas_call(
        proj_kernel,
        name="proj_gradient",
        out_shape=jax.ShapeDtypeStruct((TOK, 2 * STATE), F32),
        in_specs=[pl.BlockSpec(memory_space=pltpu.SMEM)] + [vm] * 5,
        out_specs=vm,
        compiler_params=pltpu.CompilerParams(vmem_limit_bytes=16 * MIB),
        cost_estimate=pl.CostEstimate(flops=700_000_000, bytes_accessed=4_000_000, transcendentals=0),
    )(tile, pair, proj, high, low, state)


def ring_place():
    role = lax.axis_index("seq")
    chip = lax.axis_index("dp")
    x, y = chip % 4, chip // 4 % 4
    return jnp.where(role == 0, x, y), jnp.where(role == 0, y, x)


def weight_kernel(grad_ref, other_ref, hidden_ref, wide_ref, *refs):
    outs, sums = refs[:RING], refs[RING]
    role = lax.axis_index("seq")
    own = jnp.concatenate(split2(grad_ref[...]), axis=1)
    other = jnp.concatenate(split2(other_ref[...]), axis=1)
    chunk = 256
    for c in range(HALF // chunk):
        lanes = pl.ds(pl.multiple_of(role * HALF + c * chunk, 128), chunk)
        got = dot(hidden_ref[:, lanes], own, TN)
        got = got + dot(wide_ref[:, c * chunk : (c + 1) * chunk].astype(BF16), other, TN)
        sums[c * chunk : (c + 1) * chunk, :] = got[:, : 2 * STATE] + got[:, 2 * STATE :]
    me, _ = ring_place()
    for k in range(RING):
        place = lax.rem(me + k, RING) * PIECE
        outs[k][...] = sums[pl.ds(pl.multiple_of(place, 8), PIECE), :]


def weight_call(grad, other, hidden, wide):
    vm = pl.BlockSpec(memory_space=pltpu.VMEM)
    return pl.pallas_call(
        weight_kernel,
        name="weight_gradient",
        out_shape=[jax.ShapeDtypeStruct((PIECE, 2 * STATE), F32)] * RING,
        in_specs=[vm] * 4,
        out_specs=[vm] * RING,
        scratch_shapes=[pltpu.VMEM((HALF, 2 * STATE), F32)],
        compiler_params=pltpu.CompilerParams(vmem_limit_bytes=16 * MIB),
        cost_estimate=pl.CostEstimate(flops=1_400_000_000, bytes_accessed=4_000_000, transcendentals=0),
    )(grad, other, hidden, wide)


def input_kernel(
    tile_ref, x_ref, g_ref, run_ref, cols_ref, scale_ref, step_ref, rates_ref, gain_ref, state_ref, proj_ref,
    dx_ref, dstep_ref, small_ref,
    scores, rows, mine_terms, sums, gains, slopes, direct, owns,
):
    role = lax.axis_index("seq")
    first_role = jnp.where(role == 0, 1.0, 0.0).astype(F32)
    present = jnp.where(tile_ref[0, 0] == 0, 1.0, 0.0).astype(F32)
    k = pl.program_id(0)

    @pl.when(k == 0)
    def _():
        small_ref[...] = jnp.zeros_like(small_ref)
        scores[...] = dot3(proj_ref[:, :STATE], proj_ref[:, STATE:], NT) * present
        gains[...] = jnp.broadcast_to(turn_column(gain_ref[...]), (HEADS, 128))
        mine_high, mine_low = split2(jnp.where(role == 0, proj_ref[:, :STATE], proj_ref[:, STATE:]))
        mine_terms[...] = jnp.concatenate([mine_high, mine_low, mine_high], axis=1)

    bias = causal_bias()
    state_high, state_low = split2(state_ref[...])
    carried = dot(mine_terms[...], jnp.concatenate([state_high, state_high, state_low], axis=0), NN)
    carried = carried * spread_heads(scale_ref[...], STEP_FEAT)
    select = head_rows(STEP_HEADS, STEP_HEADS, STEP_FEAT)
    at = pl.ds(pl.multiple_of(k * STEP_HEADS, STEP_HEADS), STEP_HEADS)
    gain_row = jnp.sum(select * gains[at, :1], axis=0, keepdims=True) * present
    x_all = x_ref[...].astype(F32)
    g_all = g_ref[...].astype(F32)
    own = jnp.where(role == 0, x_all, g_all)
    pick = jnp.concatenate([select, jnp.zeros_like(select)], axis=0).astype(BF16)
    own_high, own_low = split2(own * carried)
    by_own = (dot(pick, own_high, NT) + dot(pick, own_low, NT))[:STEP_HEADS]
    within = []
    for q in range(STEP_HEADS // 2):
        lanes = slice(q * 128, q * 128 + 128)
        x = x_ref[:, lanes]
        upper = jnp.zeros((STATE, 128), F32)
        lower = jnp.zeros((STATE, 128), F32)
        for half in range(2):
            r = 2 * q + half
            g = own_half(g_ref[:, lanes], half)
            d1, d2 = decays(run_ref[r : r + 1, :], cols_ref[0][:, r : r + 1], bias)
            m1 = d1 * scores[:STATE, :]
            m2 = d2 * scores[STATE:, STATE:]
            f1 = m1 * dot(x[:STATE], g, NT)
            f2 = m2 * dot(x[STATE:], g[STATE:], NT)
            sums[:STATE, r : r + 1] = jnp.sum(f1, axis=1, keepdims=True)
            sums[STATE:, r : r + 1] = jnp.sum(f2, axis=1, keepdims=True)
            f1 = jnp.sum(f1, axis=0, keepdims=True)
            f2 = jnp.sum(f2, axis=0, keepdims=True)
            rows[r : r + 1, :STATE] = f1[:, :STATE]
            rows[r : r + 1, STATE:] = f1[:, STATE:] + f2
            h1, l1 = split2(m1)
            h2, l2 = split2(m2)
            upper = upper + dot(h1, g, NN) + dot(l1, g, NN)
            lower = lower + dot(h2, g[STATE:], NN) + dot(l2, g[STATE:], NN)
        within.append(jnp.concatenate([upper, lower], axis=0))
    total = jnp.concatenate(within, axis=1) + first_role * carried
    dx_ref[...] = (total + gain_row * g_all).astype(BF16)

    r8 = lax.broadcasted_iota(jnp.int32, (8, 128), 0)
    lane = lax.broadcasted_iota(jnp.int32, (8, 128), 1)
    gx = jnp.sum(g_all * x_all, axis=0, keepdims=True) * present
    d_gain = jnp.sum(select * gx, axis=1, keepdims=True) * (1.0 / SCENES)
    small_ref[:, 128:] += jnp.where(lane == r8 + k * STEP_HEADS, d_gain, 0.0)
    columns = sums[...].T[:STEP_HEADS]
    direct[at, :] = columns + first_role * by_own
    slopes[at, :] = rows[...] - columns + (1.0 - 2.0 * first_role) * by_own
    owns[at, :] = by_own

    @pl.when(k == GROUPS - 1)
    def _():
        row = lax.broadcasted_iota(jnp.int32, (TOK, TOK), 0)
        col = lax.broadcasted_iota(jnp.int32, (TOK, TOK), 1)
        after = jnp.where(row >= col, 1.0, 0.0).astype(BF16)
        logs = sum_parts(dot(split3(slopes[...]).astype(BF16), after, NN), HEADS)
        logs = logs + first_role * jnp.sum(owns[...], axis=1, keepdims=True)
        step = step_ref[...]
        rate = rates_ref[:, :1]
        dstep_ref[...] = direct[...] / step + rate * logs
        d_rate = rate * present * jnp.sum(step * logs, axis=1, keepdims=True) * (1.0 / SCENES)
        for t in range(GROUPS):
            part = d_rate[t * STEP_HEADS : (t + 1) * STEP_HEADS]
            small_ref[:, :128] += jnp.where(lane == r8 + t * STEP_HEADS, part, 0.0)


def input_call(tile, x, g, run, cols, scale, step, rates, gain, state, proj):
    feat = pl.BlockSpec((TOK, STEP_FEAT), lambda k: (0, k))
    head = pl.BlockSpec((STEP_HEADS, TOK), lambda k: (k, 0))
    return pl.pallas_call(
        input_kernel,
        name="input_gradient",
        grid=(GROUPS,),
        out_shape=(
            jax.ShapeDtypeStruct((TOK, FEAT), BF16),
            jax.ShapeDtypeStruct((HEADS, TOK), F32),
            jax.ShapeDtypeStruct((8, 256), F32),
        ),
        in_specs=[
            pl.BlockSpec(memory_space=pltpu.SMEM),
            feat,
            feat,
            head,
            pl.BlockSpec((1, TOK, STEP_HEADS), lambda k: (k, 0, 0)),
            head,
            pl.BlockSpec((HEADS, TOK), lambda k: (0, 0)),
            pl.BlockSpec((HEADS, 128), lambda k: (0, 0)),
            pl.BlockSpec((1, HEADS), lambda k: (0, 0)),
            pl.BlockSpec((STATE, STEP_FEAT), lambda k: (0, k)),
            pl.BlockSpec((TOK, 2 * STATE), lambda k: (0, 0)),
        ],
        out_specs=(feat, pl.BlockSpec((HEADS, TOK), lambda k: (0, 0)), pl.BlockSpec((8, 256), lambda k: (0, 0))),
        scratch_shapes=[
            pltpu.VMEM((TOK, TOK), F32),
            pltpu.VMEM((STEP_HEADS, TOK), F32),
            pltpu.VMEM((TOK, 3 * STATE), BF16),
            pltpu.VMEM((TOK, 128), F32),
            pltpu.VMEM((HEADS, 128), F32),
            pltpu.VMEM((HEADS, TOK), F32),
            pltpu.VMEM((HEADS, TOK), F32),
            pltpu.VMEM((HEADS, TOK), F32),
        ],
        compiler_params=pltpu.CompilerParams(vmem_limit_bytes=16 * MIB),
        cost_estimate=pl.CostEstimate(flops=6_000_000_000, bytes_accessed=8_000_000, transcendentals=2_600_000),
    )(tile, x, g, run, cols, scale, step, rates, gain, state, proj)


def last_kernel(pieces_ref, out_ref, rate_ref, gain_ref, small, sems):
    role = lax.axis_index("seq")
    few = pltpu.make_async_copy(pieces_ref.at[:, pl.ds(ROWS, 8)], small, sems.at[PLANE])
    few.start()
    copies = []
    for j in range(PLANE):
        place = jnp.where(role == 0, j % RING * RING + j // RING, j)
        copies.append(pltpu.make_async_copy(pieces_ref.at[j, pl.ds(0, ROWS)], out_ref.at[place], sems.at[j]))
    for copy in copies:
        copy.start()
    few.wait()
    total = jnp.sum(jnp.sum(small[...], axis=0), axis=0, keepdims=True)
    share = HEADS // 2
    rate_ref[...] = jnp.where(role == 0, total[:, :share], total[:, share:HEADS])
    gain_ref[...] = jnp.where(role == 0, total[:, 128 : 128 + share], total[:, 128 + share : 128 + HEADS])
    for copy in copies:
        copy.wait()


def last_call(pieces):
    hbm = pl.BlockSpec(memory_space=pl.ANY)
    vm = pl.BlockSpec(memory_space=pltpu.VMEM)
    return pl.pallas_call(
        last_kernel,
        name="weight_rows",
        out_shape=(
            jax.ShapeDtypeStruct((PLANE, ROWS, 2 * STATE), F32),
            jax.ShapeDtypeStruct((1, HEADS // 2), F32),
            jax.ShapeDtypeStruct((1, HEADS // 2), F32),
        ),
        in_specs=[hbm],
        out_specs=(hbm, vm, vm),
        scratch_shapes=[pltpu.VMEM((PLANE, 8, 2 * STATE), F32), pltpu.SemaphoreType.DMA((PLANE + 1,))],
        compiler_params=pltpu.CompilerParams(vmem_limit_bytes=16 * MIB),
        cost_estimate=pl.CostEstimate(flops=10_000, bytes_accessed=2_600_000, transcendentals=0),
    )(pieces)


STRIDE = {"z": 16, "y": 4, "x": 1}


def moved(chip, axis, size, new):
    c = chip // STRIDE[axis] % size
    return chip + (new(c) - c) * STRIDE[axis]


def ring_shift(v, stage, k):
    pairs = []
    for core, axes in enumerate(("xy", "yx")):
        for chip in range(SCENES):
            to = moved(chip, axes[stage], RING, lambda c: (c + k) % RING)
            pairs.append((core * SCENES + chip, core * SCENES + to))
    return lax.ppermute(v, ("seq", "dp"), pairs)


def across_z(v, bit):
    return lax.ppermute(v, "dp", [(i, moved(i, "z", 8, lambda c: c ^ bit)) for i in range(SCENES)])


def swap(v):
    return lax.ppermute(v, "seq", [(0, 1), (1, 0)])


def shards(hidden, scan_input, grad_out, step_size, proj_weight, log_rate, skip_gain, tile_list):
    hid, x, g, step = hidden[0], scan_input[0], grad_out[0], step_size[0]
    proj, run, cols, scale, rates, high, low, send, wide = state_call(
        tile_list, hid, proj_weight, x, g, step, log_rate[None]
    )
    state = swap(send)
    wide = swap(wide)
    pair = pair_call(x, g, run, cols)
    grad = proj_call(tile_list, pair, proj, high, low, state)
    pieces = weight_call(grad, swap(grad), hid, wide)
    _, second = ring_place()
    sent = [ring_shift(pieces[k], 0, k) for k in range(1, RING)]
    dx, dstep, small = input_call(tile_list, x, g, run, cols, scale, step, rates, skip_gain[None], state, proj)
    sent, small = lax.optimization_barrier((sent, small))
    small = small + swap(small)
    part = pieces[0] + sent[0] + sent[1] + sent[2]
    cut = [lax.dynamic_slice_in_dim(part, (second + k) % RING * ROWS, ROWS, 0) for k in range(RING)]
    part = cut[0] + sum(ring_shift(cut[k], 1, k) for k in range(1, RING))
    part = jnp.concatenate([part, small], axis=0)
    for bit in (1, 2, 6):
        part = part + across_z(part, bit)
    plane = [[z * PLANE + i for i in range(PLANE)] for z in range(SCENES // PLANE)]
    pieces = lax.all_to_all(
        jnp.broadcast_to(part, (PLANE,) + part.shape), "dp", 0, 0, axis_index_groups=plane, tiled=True
    )
    grad_weight, d_rate, d_gain = last_call(pieces)
    grad_weight = grad_weight.reshape(HALF, 2 * STATE)
    return dx[None], dstep[None], grad_weight, d_rate[0], d_gain[0]


def solution(mesh):
    in_specs = (
        P("dp", "seq", None),
        P("dp", "seq", None),
        P("dp", "seq", None),
        P("dp", None, "seq"),
        P(),
        P(),
        P(),
        P("dp", "seq"),
    )
    out_specs = (P("dp", "seq", None), P("dp", None, "seq"), P("seq", None), P("seq"), P("seq"))
    return jax.shard_map(shards, mesh=mesh, in_specs=in_specs, out_specs=out_specs, check_vma=False)
```

```python
import jax
import jax.numpy as jnp
from jax import lax
from jax.experimental import pallas as pl
from jax.experimental.pallas import tpu as pltpu
from jax.sharding import PartitionSpec as P

F32 = jnp.float32
BF16 = jnp.bfloat16
HEADS = 40
WIDTH = 64
STATE = 128
TOK = 256
FEAT = HEADS * WIDTH
SCENES = 128
STEP_HEADS = 8
GROUPS = HEADS // STEP_HEADS
STEP_FEAT = STEP_HEADS * WIDTH
HALF = FEAT // 2
MIB = 1024 * 1024
RING = 4
PIECE = HALF // RING
PLANE = RING * RING
ROWS = HALF // PLANE

NN = (((1,), (0,)), ((), ()))
NT = (((1,), (1,)), ((), ()))
TN = (((0,), (0,)), ((), ()))


def dot(a, b, dims):
    return lax.dot_general(a, b, dims, preferred_element_type=F32)


def split2(v):
    high = v.astype(BF16)
    return high, (v - high.astype(F32)).astype(BF16)


def split3(v):
    rows = v.shape[0]
    high = v.astype(BF16).astype(F32)
    rest = v - high
    mid = rest.astype(BF16).astype(F32)
    low = rest - mid
    parts = [high, mid, low]
    extra = -3 * rows % 16
    if extra:
        parts.append(jnp.zeros((extra, v.shape[1]), F32))
    return jnp.concatenate(parts, axis=0)


def dot3(a, b, dims):
    ah, al = split2(a)
    bh, bl = split2(b)
    return dot(ah, bh, dims) + dot(al, bh, dims) + dot(ah, bl, dims)


def head_rows(rows, heads, width):
    row = lax.broadcasted_iota(jnp.int32, (rows, width), 0)
    head = lax.broadcasted_iota(jnp.int32, (rows, width), 1) // WIDTH
    hit = (head == row) | (head == row - heads) | (head == row - 2 * heads)
    return jnp.where(hit & (row < 3 * heads), 1.0, 0.0)


def spread_heads(v, width):
    parts = split3(v).astype(BF16)
    return dot(parts, head_rows(parts.shape[0], v.shape[0], width).astype(BF16), TN)


def turn_column(row):
    same = lax.broadcasted_iota(jnp.int32, (HEADS, HEADS), 0) == lax.broadcasted_iota(jnp.int32, (HEADS, HEADS), 1)
    return jnp.sum(jnp.where(same, row, 0.0), axis=1, keepdims=True)


def sum_parts(v, heads):
    return v[:heads] + v[heads : 2 * heads] + v[2 * heads : 3 * heads]


def state_kernel(
    tile_ref, hidden_hbm, weight_hbm, x_hbm, g_hbm, step_hbm, rate_ref,
    proj_ref, run_ref, cols_ref, scale_ref, rates_ref, high_ref, low_ref, send_ref, wide_ref,
    hidden, weight, values, step_vm, sems,
):
    role = lax.axis_index("seq")
    take_step = pltpu.make_async_copy(step_hbm, step_vm, sems.at[2 * GROUPS + 1])
    take_step.start()
    copies = []
    for c in range(GROUPS):
        part = pl.ds(c * STEP_FEAT, STEP_FEAT)
        copies.append(pltpu.make_async_copy(hidden_hbm.at[:, part], hidden.at[:, part], sems.at[c]))
        copies.append(pltpu.make_async_copy(weight_hbm.at[part], weight.at[part], sems.at[GROUPS + c]))
    for copy in copies:
        copy.start()
    take_x = pltpu.make_async_copy(x_hbm, values, sems.at[2 * GROUPS])
    take_g = pltpu.make_async_copy(g_hbm, values, sems.at[2 * GROUPS])

    @pl.when(role == 0)
    def _():
        take_x.start()

    @pl.when(role != 0)
    def _():
        take_g.start()

    present = jnp.where(tile_ref[0, 0] == 0, 1.0, 0.0).astype(F32)
    take_step.wait()
    step = step_vm[...]
    rate = -jnp.exp(turn_column(rate_ref[...]))
    rates_ref[...] = jnp.broadcast_to(rate, (HEADS, 128))
    logs = step * present * rate
    row = lax.broadcasted_iota(jnp.int32, (TOK, TOK), 0)
    col = lax.broadcasted_iota(jnp.int32, (TOK, TOK), 1)
    upto = jnp.where(row <= col, 1.0, 0.0).astype(BF16)
    run = sum_parts(dot(split3(logs).astype(BF16), upto, NN), HEADS)
    run_ref[...] = run
    less = run - jnp.log(step)
    turned = jnp.concatenate([less, jnp.zeros((STATE - HEADS, TOK), F32)], axis=0).T
    for k in range(GROUPS):
        cols_ref[k] = turned[:, k * STEP_HEADS : (k + 1) * STEP_HEADS]
    tail = step * jnp.exp(run[:, TOK - 1 :] - run)
    scale = jnp.where(role == 0, tail, jnp.exp(run)) * present
    scale_ref[...] = scale

    proj = jnp.zeros((TOK, 2 * STATE), F32)
    for c in range(GROUPS):
        copies[2 * c].wait()
        copies[2 * c + 1].wait()
        part = slice(c * STEP_FEAT, (c + 1) * STEP_FEAT)
        proj = proj + dot(hidden[:, part], weight[part, :], NN)
    proj_ref[...] = proj
    mine = jnp.where(role == 0, proj[:, :STATE], proj[:, STATE:])
    mine_high, mine_low = split2(mine)
    take_x.wait()
    parts = split3(scale).astype(BF16)
    for c in range(GROUPS):
        part = slice(c * STEP_FEAT, (c + 1) * STEP_FEAT)
        r = lax.broadcasted_iota(jnp.int32, (parts.shape[0], STEP_FEAT), 0)
        h = lax.broadcasted_iota(jnp.int32, (parts.shape[0], STEP_FEAT), 1) // WIDTH + c * STEP_HEADS
        hit = (h == r) | (h == r - HEADS) | (h == r - 2 * HEADS)
        pick = jnp.where(hit, 1.0, 0.0).astype(BF16)
        scaled = dot(parts, pick, TN) * values[:, part].astype(F32)
        high, low = split2(scaled)
        high_ref[:, part] = high
        low_ref[:, part] = low
        send_ref[:, part] = dot(mine_high, high, TN) + dot(mine_low, high, TN) + dot(mine_high, low, TN)
    for c in range(GROUPS):
        lanes = pl.ds(pl.multiple_of((1 - role) * HALF + c * 256, 128), 256)
        wide_ref[:, c * 256 : (c + 1) * 256] = hidden[:, lanes].astype(F32)


def state_call(tile, hidden, weight, x, g, step, log_rate):
    sm = pl.BlockSpec(memory_space=pltpu.SMEM)
    vm = pl.BlockSpec(memory_space=pltpu.VMEM)
    hbm = pl.BlockSpec(memory_space=pltpu.HBM)
    return pl.pallas_call(
        state_kernel,
        name="state_to_send",
        out_shape=(
            jax.ShapeDtypeStruct((TOK, 2 * STATE), F32),
            jax.ShapeDtypeStruct((HEADS, TOK), F32),
            jax.ShapeDtypeStruct((GROUPS, TOK, STEP_HEADS), F32),
            jax.ShapeDtypeStruct((HEADS, TOK), F32),
            jax.ShapeDtypeStruct((HEADS, 128), F32),
            jax.ShapeDtypeStruct((TOK, FEAT), BF16),
            jax.ShapeDtypeStruct((TOK, FEAT), BF16),
            jax.ShapeDtypeStruct((STATE, FEAT), F32),
            jax.ShapeDtypeStruct((TOK, HALF), F32),
        ),
        in_specs=[sm] + [hbm] * 5 + [vm],
        out_specs=(vm,) * 9,
        scratch_shapes=[
            pltpu.VMEM((TOK, FEAT), BF16),
            pltpu.VMEM((FEAT, 2 * STATE), BF16),
            pltpu.VMEM((TOK, FEAT), BF16),
            pltpu.VMEM((HEADS, TOK), F32),
            pltpu.SemaphoreType.DMA((2 * GROUPS + 2,)),
        ],
        compiler_params=pltpu.CompilerParams(vmem_limit_bytes=48 * MIB),
        cost_estimate=pl.CostEstimate(flops=1_000_000_000, bytes_accessed=8_000_000, transcendentals=20_000),
    )(tile, hidden, weight, x, g, step, log_rate)


def causal_bias():
    row = lax.broadcasted_iota(jnp.int32, (STATE, STATE), 0)
    col = lax.broadcasted_iota(jnp.int32, (STATE, STATE), 1)
    return jnp.where(col >= row, 0.0, -1e30).astype(F32)


def own_half(v, which):
    lane = lax.broadcasted_iota(jnp.int32, v.shape, 1)
    keep = (lane < WIDTH) if which == 0 else (lane >= WIDTH)
    return jnp.where(keep, v, jnp.zeros_like(v))


def decays(run_row, less_col, bias):
    d = run_row - less_col
    first = jnp.exp(jnp.concatenate([d[:STATE, :STATE] + bias, d[:STATE, STATE:]], axis=1))
    second = jnp.exp(d[STATE:, STATE:] + bias)
    return first, second


def pair_kernel(x_ref, g_ref, run_ref, cols_ref, out_ref):
    bias = causal_bias()
    first = jnp.zeros((STATE, TOK), F32)
    second = jnp.zeros((STATE, STATE), F32)
    for q in range(STEP_HEADS // 2):
        lanes = slice(q * 128, q * 128 + 128)
        x, g = x_ref[:, lanes], g_ref[:, lanes]
        w = dot(jnp.concatenate([own_half(x, 0), own_half(x, 1)], axis=0), g, NT)
        for half in range(2):
            r = 2 * q + half
            d1, d2 = decays(run_ref[r : r + 1, :], cols_ref[0][:, r : r + 1], bias)
            first = first + d1 * w[half * TOK : half * TOK + STATE]
            second = second + d2 * w[half * TOK + STATE : half * TOK + TOK, STATE:]

    @pl.when(pl.program_id(0) == 0)
    def _():
        out_ref[...] = jnp.zeros_like(out_ref)

    out_ref[:STATE, :] += first
    out_ref[STATE:, STATE:] += second


def pair_call(x, g, run, cols):
    return pl.pallas_call(
        pair_kernel,
        name="score_gradient",
        grid=(GROUPS,),
        out_shape=jax.ShapeDtypeStruct((TOK, TOK), F32),
        in_specs=[
            pl.BlockSpec((TOK, STEP_FEAT), lambda k: (0, k)),
            pl.BlockSpec((TOK, STEP_FEAT), lambda k: (0, k)),
            pl.BlockSpec((STEP_HEADS, TOK), lambda k: (k, 0)),
            pl.BlockSpec((1, TOK, STEP_HEADS), lambda k: (k, 0, 0)),
        ],
        out_specs=pl.BlockSpec((TOK, TOK), lambda k: (0, 0)),
        compiler_params=pltpu.CompilerParams(vmem_limit_bytes=16 * MIB),
        cost_estimate=pl.CostEstimate(flops=1_500_000_000, bytes_accessed=3_000_000, transcendentals=2_600_000),
    )(x, g, run, cols)


def proj_kernel(tile_ref, pair_ref, proj_ref, high_ref, low_ref, state_ref, grad_ref):
    role = lax.axis_index("seq")
    present = jnp.where(tile_ref[0, 0] == 0, 1.0, 0.0).astype(F32)
    pair = pair_ref[...] * present
    proj = proj_ref[...]
    keys = dot3(pair, proj[:, STATE:], NN)
    query = dot3(pair, proj[:, :STATE], TN)
    both = jnp.concatenate(split2(state_ref[...]), axis=0)
    high = dot(high_ref[...], both, NT)
    across = high[:, :STATE] + high[:, STATE:] + dot(low_ref[...], both[:STATE], NT)
    keys = keys + jnp.where(role == 0, across, 0.0)
    query = query + jnp.where(role == 0, 0.0, across)
    grad_ref[...] = jnp.concatenate([keys, query], axis=1) * (1.0 / SCENES)


def proj_call(tile, pair, proj, high, low, state):
    vm = pl.BlockSpec(memory_space=pltpu.VMEM)
    return pl.pallas_call(
        proj_kernel,
        name="proj_gradient",
        out_shape=jax.ShapeDtypeStruct((TOK, 2 * STATE), F32),
        in_specs=[pl.BlockSpec(memory_space=pltpu.SMEM)] + [vm] * 5,
        out_specs=vm,
        compiler_params=pltpu.CompilerParams(vmem_limit_bytes=16 * MIB),
        cost_estimate=pl.CostEstimate(flops=700_000_000, bytes_accessed=4_000_000, transcendentals=0),
    )(tile, pair, proj, high, low, state)


def ring_place():
    role = lax.axis_index("seq")
    chip = lax.axis_index("dp")
    x, y = chip % 4, chip // 4 % 4
    return jnp.where(role == 0, x, y), jnp.where(role == 0, y, x)


def weight_kernel(grad_ref, other_ref, hidden_ref, wide_ref, *refs):
    outs, sums = refs[:RING], refs[RING]
    role = lax.axis_index("seq")
    own = jnp.concatenate(split2(grad_ref[...]), axis=1)
    other = jnp.concatenate(split2(other_ref[...]), axis=1)
    chunk = 256
    for c in range(HALF // chunk):
        lanes = pl.ds(pl.multiple_of(role * HALF + c * chunk, 128), chunk)
        got = dot(hidden_ref[:, lanes], own, TN)
        got = got + dot(wide_ref[:, c * chunk : (c + 1) * chunk].astype(BF16), other, TN)
        sums[c * chunk : (c + 1) * chunk, :] = got[:, : 2 * STATE] + got[:, 2 * STATE :]
    me, _ = ring_place()
    for k in range(RING):
        place = lax.rem(me + k, RING) * PIECE
        outs[k][...] = sums[pl.ds(pl.multiple_of(place, 8), PIECE), :]


def weight_call(grad, other, hidden, wide):
    vm = pl.BlockSpec(memory_space=pltpu.VMEM)
    return pl.pallas_call(
        weight_kernel,
        name="weight_gradient",
        out_shape=[jax.ShapeDtypeStruct((PIECE, 2 * STATE), F32)] * RING,
        in_specs=[vm] * 4,
        out_specs=[vm] * RING,
        scratch_shapes=[pltpu.VMEM((HALF, 2 * STATE), F32)],
        compiler_params=pltpu.CompilerParams(vmem_limit_bytes=16 * MIB),
        cost_estimate=pl.CostEstimate(flops=1_400_000_000, bytes_accessed=4_000_000, transcendentals=0),
    )(grad, other, hidden, wide)


def input_kernel(
    tile_ref, x_ref, g_ref, run_ref, cols_ref, scale_ref, step_ref, rates_ref, gain_ref, state_ref, proj_ref,
    dx_ref, dstep_ref, small_ref,
    scores, rows, mine_terms, sums, gains, slopes, direct, owns,
):
    role = lax.axis_index("seq")
    first_role = jnp.where(role == 0, 1.0, 0.0).astype(F32)
    present = jnp.where(tile_ref[0, 0] == 0, 1.0, 0.0).astype(F32)
    k = pl.program_id(0)

    @pl.when(k == 0)
    def _():
        small_ref[...] = jnp.zeros_like(small_ref)
        scores[...] = dot3(proj_ref[:, :STATE], proj_ref[:, STATE:], NT) * present
        gains[...] = jnp.broadcast_to(turn_column(gain_ref[...]), (HEADS, 128))
        mine_high, mine_low = split2(jnp.where(role == 0, proj_ref[:, :STATE], proj_ref[:, STATE:]))
        mine_terms[...] = jnp.concatenate([mine_high, mine_low, mine_high], axis=1)

    bias = causal_bias()
    state_high, state_low = split2(state_ref[...])
    carried = dot(mine_terms[...], jnp.concatenate([state_high, state_high, state_low], axis=0), NN)
    carried = carried * spread_heads(scale_ref[...], STEP_FEAT)
    select = head_rows(STEP_HEADS, STEP_HEADS, STEP_FEAT)
    at = pl.ds(pl.multiple_of(k * STEP_HEADS, STEP_HEADS), STEP_HEADS)
    gain_row = jnp.sum(select * gains[at, :1], axis=0, keepdims=True) * present
    x_all = x_ref[...].astype(F32)
    g_all = g_ref[...].astype(F32)
    own = jnp.where(role == 0, x_all, g_all)
    pick = jnp.concatenate([select, jnp.zeros_like(select)], axis=0).astype(BF16)
    own_high, own_low = split2(own * carried)
    by_own = (dot(pick, own_high, NT) + dot(pick, own_low, NT))[:STEP_HEADS]
    within = []
    for q in range(STEP_HEADS // 2):
        lanes = slice(q * 128, q * 128 + 128)
        x = x_ref[:, lanes]
        upper = jnp.zeros((STATE, 128), F32)
        lower = jnp.zeros((STATE, 128), F32)
        for half in range(2):
            r = 2 * q + half
            g = own_half(g_ref[:, lanes], half)
            d1, d2 = decays(run_ref[r : r + 1, :], cols_ref[0][:, r : r + 1], bias)
            m1 = d1 * scores[:STATE, :]
            m2 = d2 * scores[STATE:, STATE:]
            f1 = m1 * dot(x[:STATE], g, NT)
            f2 = m2 * dot(x[STATE:], g[STATE:], NT)
            sums[:STATE, r : r + 1] = jnp.sum(f1, axis=1, keepdims=True)
            sums[STATE:, r : r + 1] = jnp.sum(f2, axis=1, keepdims=True)
            f1 = jnp.sum(f1, axis=0, keepdims=True)
            f2 = jnp.sum(f2, axis=0, keepdims=True)
            rows[r : r + 1, :STATE] = f1[:, :STATE]
            rows[r : r + 1, STATE:] = f1[:, STATE:] + f2
            h1, l1 = split2(m1)
            h2, l2 = split2(m2)
            upper = upper + dot(h1, g, NN) + dot(l1, g, NN)
            lower = lower + dot(h2, g[STATE:], NN) + dot(l2, g[STATE:], NN)
        within.append(jnp.concatenate([upper, lower], axis=0))
    total = jnp.concatenate(within, axis=1) + first_role * carried
    dx_ref[...] = (total + gain_row * g_all).astype(BF16)

    r8 = lax.broadcasted_iota(jnp.int32, (8, 128), 0)
    lane = lax.broadcasted_iota(jnp.int32, (8, 128), 1)
    gx = jnp.sum(g_all * x_all, axis=0, keepdims=True) * present
    d_gain = jnp.sum(select * gx, axis=1, keepdims=True) * (1.0 / SCENES)
    small_ref[:, 128:] += jnp.where(lane == r8 + k * STEP_HEADS, d_gain, 0.0)
    columns = sums[...].T[:STEP_HEADS]
    direct[at, :] = columns + first_role * by_own
    slopes[at, :] = rows[...] - columns + (1.0 - 2.0 * first_role) * by_own
    owns[at, :] = by_own

    @pl.when(k == GROUPS - 1)
    def _():
        row = lax.broadcasted_iota(jnp.int32, (TOK, TOK), 0)
        col = lax.broadcasted_iota(jnp.int32, (TOK, TOK), 1)
        after = jnp.where(row >= col, 1.0, 0.0).astype(BF16)
        logs = sum_parts(dot(split3(slopes[...]).astype(BF16), after, NN), HEADS)
        logs = logs + first_role * jnp.sum(owns[...], axis=1, keepdims=True)
        step = step_ref[...]
        rate = rates_ref[:, :1]
        dstep_ref[...] = direct[...] / step + rate * logs
        d_rate = rate * present * jnp.sum(step * logs, axis=1, keepdims=True) * (1.0 / SCENES)
        for t in range(GROUPS):
            part = d_rate[t * STEP_HEADS : (t + 1) * STEP_HEADS]
            small_ref[:, :128] += jnp.where(lane == r8 + t * STEP_HEADS, part, 0.0)


def input_call(tile, x, g, run, cols, scale, step, rates, gain, state, proj):
    feat = pl.BlockSpec((TOK, STEP_FEAT), lambda k: (0, k))
    head = pl.BlockSpec((STEP_HEADS, TOK), lambda k: (k, 0))
    return pl.pallas_call(
        input_kernel,
        name="input_gradient",
        grid=(GROUPS,),
        out_shape=(
            jax.ShapeDtypeStruct((TOK, FEAT), BF16),
            jax.ShapeDtypeStruct((HEADS, TOK), F32),
            jax.ShapeDtypeStruct((8, 256), F32),
        ),
        in_specs=[
            pl.BlockSpec(memory_space=pltpu.SMEM),
            feat,
            feat,
            head,
            pl.BlockSpec((1, TOK, STEP_HEADS), lambda k: (k, 0, 0)),
            head,
            pl.BlockSpec((HEADS, TOK), lambda k: (0, 0)),
            pl.BlockSpec((HEADS, 128), lambda k: (0, 0)),
            pl.BlockSpec((1, HEADS), lambda k: (0, 0)),
            pl.BlockSpec((STATE, STEP_FEAT), lambda k: (0, k)),
            pl.BlockSpec((TOK, 2 * STATE), lambda k: (0, 0)),
        ],
        out_specs=(feat, pl.BlockSpec((HEADS, TOK), lambda k: (0, 0)), pl.BlockSpec((8, 256), lambda k: (0, 0))),
        scratch_shapes=[
            pltpu.VMEM((TOK, TOK), F32),
            pltpu.VMEM((STEP_HEADS, TOK), F32),
            pltpu.VMEM((TOK, 3 * STATE), BF16),
            pltpu.VMEM((TOK, 128), F32),
            pltpu.VMEM((HEADS, 128), F32),
            pltpu.VMEM((HEADS, TOK), F32),
            pltpu.VMEM((HEADS, TOK), F32),
            pltpu.VMEM((HEADS, TOK), F32),
        ],
        compiler_params=pltpu.CompilerParams(vmem_limit_bytes=16 * MIB),
        cost_estimate=pl.CostEstimate(flops=6_000_000_000, bytes_accessed=8_000_000, transcendentals=2_600_000),
    )(tile, x, g, run, cols, scale, step, rates, gain, state, proj)


def last_kernel(pieces_ref, out_ref, rate_ref, gain_ref, small, sems):
    role = lax.axis_index("seq")
    few = pltpu.make_async_copy(pieces_ref.at[:, pl.ds(ROWS, 8)], small, sems.at[PLANE])
    few.start()
    copies = []
    for j in range(PLANE):
        place = jnp.where(role == 0, j % RING * RING + j // RING, j)
        copies.append(pltpu.make_async_copy(pieces_ref.at[j, pl.ds(0, ROWS)], out_ref.at[place], sems.at[j]))
    for copy in copies:
        copy.start()
    few.wait()
    total = jnp.sum(jnp.sum(small[...], axis=0), axis=0, keepdims=True)
    share = HEADS // 2
    rate_ref[...] = jnp.where(role == 0, total[:, :share], total[:, share:HEADS])
    gain_ref[...] = jnp.where(role == 0, total[:, 128 : 128 + share], total[:, 128 + share : 128 + HEADS])
    for copy in copies:
        copy.wait()


def last_call(pieces):
    hbm = pl.BlockSpec(memory_space=pl.ANY)
    vm = pl.BlockSpec(memory_space=pltpu.VMEM)
    return pl.pallas_call(
        last_kernel,
        name="weight_rows",
        out_shape=(
            jax.ShapeDtypeStruct((PLANE, ROWS, 2 * STATE), F32),
            jax.ShapeDtypeStruct((1, HEADS // 2), F32),
            jax.ShapeDtypeStruct((1, HEADS // 2), F32),
        ),
        in_specs=[hbm],
        out_specs=(hbm, vm, vm),
        scratch_shapes=[pltpu.VMEM((PLANE, 8, 2 * STATE), F32), pltpu.SemaphoreType.DMA((PLANE + 1,))],
        compiler_params=pltpu.CompilerParams(vmem_limit_bytes=16 * MIB),
        cost_estimate=pl.CostEstimate(flops=10_000, bytes_accessed=2_600_000, transcendentals=0),
    )(pieces)


STRIDE = {"z": 16, "y": 4, "x": 1}


def moved(chip, axis, size, new):
    c = chip // STRIDE[axis] % size
    return chip + (new(c) - c) * STRIDE[axis]


def ring_shift(v, stage, k):
    pairs = []
    for core, axes in enumerate(("xy", "yx")):
        for chip in range(SCENES):
            to = moved(chip, axes[stage], RING, lambda c: (c + k) % RING)
            pairs.append((core * SCENES + chip, core * SCENES + to))
    return lax.ppermute(v, ("seq", "dp"), pairs)


def across_z(v, bit):
    return lax.ppermute(v, "dp", [(i, moved(i, "z", 8, lambda c: c ^ bit)) for i in range(SCENES)])


def swap(v):
    return lax.ppermute(v, "seq", [(0, 1), (1, 0)])


def shards(hidden, scan_input, grad_out, step_size, proj_weight, log_rate, skip_gain, tile_list):
    hid, x, g, step = hidden[0], scan_input[0], grad_out[0], step_size[0]
    proj, run, cols, scale, rates, high, low, send, wide = state_call(
        tile_list, hid, proj_weight, x, g, step, log_rate[None]
    )
    state = swap(send)
    wide = swap(wide)
    pair = pair_call(x, g, run, cols)
    grad = proj_call(tile_list, pair, proj, high, low, state)
    pieces = weight_call(grad, swap(grad), hid, wide)
    _, second = ring_place()
    sent = [ring_shift(pieces[k], 0, k) for k in range(1, RING)]
    dx, dstep, small = input_call(tile_list, x, g, run, cols, scale, step, rates, skip_gain[None], state, proj)
    small_own = small
    part = pieces[0] + sent[0] + sent[1] + sent[2]
    part, small_own = lax.optimization_barrier((part, small_own))
    small = small_own + swap(small_own)
    cut = [lax.dynamic_slice_in_dim(part, (second + k) % RING * ROWS, ROWS, 0) for k in range(RING)]
    part = cut[0] + sum(ring_shift(cut[k], 1, k) for k in range(1, RING))
    part = jnp.concatenate([part, small], axis=0)
    for bit in (1, 2, 6):
        part = part + across_z(part, bit)
    plane = [[z * PLANE + i for i in range(PLANE)] for z in range(SCENES // PLANE)]
    pieces = lax.all_to_all(
        jnp.broadcast_to(part, (PLANE,) + part.shape), "dp", 0, 0, axis_index_groups=plane, tiled=True
    )
    grad_weight, d_rate, d_gain = last_call(pieces)
    grad_weight = grad_weight.reshape(HALF, 2 * STATE)
    return dx[None], dstep[None], grad_weight, d_rate[0], d_gain[0]


def solution(mesh):
    in_specs = (
        P("dp", "seq", None),
        P("dp", "seq", None),
        P("dp", "seq", None),
        P("dp", None, "seq"),
        P(),
        P(),
        P(),
        P("dp", "seq"),
    )
    out_specs = (P("dp", "seq", None), P("dp", None, "seq"), P("seq", None), P("seq"), P("seq"))
    return jax.shard_map(shards, mesh=mesh, in_specs=in_specs, out_specs=out_specs, check_vma=False)
```

```python
import jax
import jax.numpy as jnp
from jax import lax
from jax.experimental import pallas as pl
from jax.experimental.pallas import tpu as pltpu
from jax.sharding import PartitionSpec as P

F32 = jnp.float32
BF16 = jnp.bfloat16
HEADS = 40
WIDTH = 64
STATE = 128
TOK = 256
FEAT = HEADS * WIDTH
SCENES = 128
STEP_HEADS = 8
GROUPS = HEADS // STEP_HEADS
STEP_FEAT = STEP_HEADS * WIDTH
HALF = FEAT // 2
MIB = 1024 * 1024
RING = 4
PIECE = HALF // RING
PLANE = RING * RING
ROWS = HALF // PLANE

NN = (((1,), (0,)), ((), ()))
NT = (((1,), (1,)), ((), ()))
TN = (((0,), (0,)), ((), ()))


def dot(a, b, dims):
    return lax.dot_general(a, b, dims, preferred_element_type=F32)


def split2(v):
    high = v.astype(BF16)
    return high, (v - high.astype(F32)).astype(BF16)


def split3(v):
    rows = v.shape[0]
    high = v.astype(BF16).astype(F32)
    rest = v - high
    mid = rest.astype(BF16).astype(F32)
    low = rest - mid
    parts = [high, mid, low]
    extra = -3 * rows % 16
    if extra:
        parts.append(jnp.zeros((extra, v.shape[1]), F32))
    return jnp.concatenate(parts, axis=0)


def dot3(a, b, dims):
    ah, al = split2(a)
    bh, bl = split2(b)
    return dot(ah, bh, dims) + dot(al, bh, dims) + dot(ah, bl, dims)


def head_rows(rows, heads, width):
    row = lax.broadcasted_iota(jnp.int32, (rows, width), 0)
    head = lax.broadcasted_iota(jnp.int32, (rows, width), 1) // WIDTH
    hit = (head == row) | (head == row - heads) | (head == row - 2 * heads)
    return jnp.where(hit & (row < 3 * heads), 1.0, 0.0)


def spread_heads(v, width):
    parts = split3(v).astype(BF16)
    return dot(parts, head_rows(parts.shape[0], v.shape[0], width).astype(BF16), TN)


def turn_column(row):
    same = lax.broadcasted_iota(jnp.int32, (HEADS, HEADS), 0) == lax.broadcasted_iota(jnp.int32, (HEADS, HEADS), 1)
    return jnp.sum(jnp.where(same, row, 0.0), axis=1, keepdims=True)


def sum_parts(v, heads):
    return v[:heads] + v[heads : 2 * heads] + v[2 * heads : 3 * heads]


def state_kernel(
    tile_ref, hidden_hbm, weight_hbm, x_hbm, g_hbm, step_hbm, rate_ref,
    proj_ref, run_ref, cols_ref, scale_ref, rates_ref, high_ref, low_ref, send_ref, wide_ref,
    hidden, weight, values, step_vm, sems,
):
    role = lax.axis_index("seq")
    take_step = pltpu.make_async_copy(step_hbm, step_vm, sems.at[2 * GROUPS + 1])
    take_step.start()
    copies = []
    for c in range(GROUPS):
        part = pl.ds(c * STEP_FEAT, STEP_FEAT)
        copies.append(pltpu.make_async_copy(hidden_hbm.at[:, part], hidden.at[:, part], sems.at[c]))
        copies.append(pltpu.make_async_copy(weight_hbm.at[part], weight.at[part], sems.at[GROUPS + c]))
    for copy in copies:
        copy.start()
    take_x = pltpu.make_async_copy(x_hbm, values, sems.at[2 * GROUPS])
    take_g = pltpu.make_async_copy(g_hbm, values, sems.at[2 * GROUPS])

    @pl.when(role == 0)
    def _():
        take_x.start()

    @pl.when(role != 0)
    def _():
        take_g.start()

    present = jnp.where(tile_ref[0, 0] == 0, 1.0, 0.0).astype(F32)
    take_step.wait()
    step = step_vm[...]
    rate = -jnp.exp(turn_column(rate_ref[...]))
    rates_ref[...] = jnp.broadcast_to(rate, (HEADS, 128))
    logs = step * present * rate
    row = lax.broadcasted_iota(jnp.int32, (TOK, TOK), 0)
    col = lax.broadcasted_iota(jnp.int32, (TOK, TOK), 1)
    upto = jnp.where(row <= col, 1.0, 0.0).astype(BF16)
    run = sum_parts(dot(split3(logs).astype(BF16), upto, NN), HEADS)
    run_ref[...] = run
    less = run - jnp.log(step)
    turned = jnp.concatenate([less, jnp.zeros((STATE - HEADS, TOK), F32)], axis=0).T
    for k in range(GROUPS):
        cols_ref[k] = turned[:, k * STEP_HEADS : (k + 1) * STEP_HEADS]
    tail = step * jnp.exp(run[:, TOK - 1 :] - run)
    scale = jnp.where(role == 0, tail, jnp.exp(run)) * present
    scale_ref[...] = scale

    proj = jnp.zeros((TOK, 2 * STATE), F32)
    for c in range(GROUPS):
        copies[2 * c].wait()
        copies[2 * c + 1].wait()
        part = slice(c * STEP_FEAT, (c + 1) * STEP_FEAT)
        proj = proj + dot(hidden[:, part], weight[part, :], NN)
    proj_ref[...] = proj
    mine = jnp.where(role == 0, proj[:, :STATE], proj[:, STATE:])
    mine_high, mine_low = split2(mine)
    take_x.wait()
    parts = split3(scale).astype(BF16)
    for c in range(GROUPS):
        part = slice(c * STEP_FEAT, (c + 1) * STEP_FEAT)
        r = lax.broadcasted_iota(jnp.int32, (parts.shape[0], STEP_FEAT), 0)
        h = lax.broadcasted_iota(jnp.int32, (parts.shape[0], STEP_FEAT), 1) // WIDTH + c * STEP_HEADS
        hit = (h == r) | (h == r - HEADS) | (h == r - 2 * HEADS)
        pick = jnp.where(hit, 1.0, 0.0).astype(BF16)
        scaled = dot(parts, pick, TN) * values[:, part].astype(F32)
        high, low = split2(scaled)
        high_ref[:, part] = high
        low_ref[:, part] = low
        send_ref[:, part] = dot(mine_high, high, TN) + dot(mine_low, high, TN) + dot(mine_high, low, TN)
    for c in range(GROUPS):
        lanes = pl.ds(pl.multiple_of((1 - role) * HALF + c * 256, 128), 256)
        wide_ref[:, c * 256 : (c + 1) * 256] = hidden[:, lanes].astype(F32)


def state_call(tile, hidden, weight, x, g, step, log_rate):
    sm = pl.BlockSpec(memory_space=pltpu.SMEM)
    vm = pl.BlockSpec(memory_space=pltpu.VMEM)
    hbm = pl.BlockSpec(memory_space=pltpu.HBM)
    return pl.pallas_call(
        state_kernel,
        name="state_to_send",
        out_shape=(
            jax.ShapeDtypeStruct((TOK, 2 * STATE), F32),
            jax.ShapeDtypeStruct((HEADS, TOK), F32),
            jax.ShapeDtypeStruct((GROUPS, TOK, STEP_HEADS), F32),
            jax.ShapeDtypeStruct((HEADS, TOK), F32),
            jax.ShapeDtypeStruct((HEADS, 128), F32),
            jax.ShapeDtypeStruct((TOK, FEAT), BF16),
            jax.ShapeDtypeStruct((TOK, FEAT), BF16),
            jax.ShapeDtypeStruct((STATE, FEAT), F32),
            jax.ShapeDtypeStruct((TOK, HALF), F32),
        ),
        in_specs=[sm] + [hbm] * 5 + [vm],
        out_specs=(vm,) * 9,
        scratch_shapes=[
            pltpu.VMEM((TOK, FEAT), BF16),
            pltpu.VMEM((FEAT, 2 * STATE), BF16),
            pltpu.VMEM((TOK, FEAT), BF16),
            pltpu.VMEM((HEADS, TOK), F32),
            pltpu.SemaphoreType.DMA((2 * GROUPS + 2,)),
        ],
        compiler_params=pltpu.CompilerParams(vmem_limit_bytes=48 * MIB),
        cost_estimate=pl.CostEstimate(flops=1_000_000_000, bytes_accessed=8_000_000, transcendentals=20_000),
    )(tile, hidden, weight, x, g, step, log_rate)


def causal_bias():
    row = lax.broadcasted_iota(jnp.int32, (STATE, STATE), 0)
    col = lax.broadcasted_iota(jnp.int32, (STATE, STATE), 1)
    return jnp.where(col >= row, 0.0, -1e30).astype(F32)


def own_half(v, which):
    lane = lax.broadcasted_iota(jnp.int32, v.shape, 1)
    keep = (lane < WIDTH) if which == 0 else (lane >= WIDTH)
    return jnp.where(keep, v, jnp.zeros_like(v))


def decays(run_row, less_col, bias):
    d = run_row - less_col
    first = jnp.exp(jnp.concatenate([d[:STATE, :STATE] + bias, d[:STATE, STATE:]], axis=1))
    second = jnp.exp(d[STATE:, STATE:] + bias)
    return first, second


def pair_kernel(x_ref, g_ref, run_ref, cols_ref, out_ref):
    bias = causal_bias()
    first = jnp.zeros((STATE, TOK), F32)
    second = jnp.zeros((STATE, STATE), F32)
    for q in range(STEP_HEADS // 2):
        lanes = slice(q * 128, q * 128 + 128)
        x, g = x_ref[:, lanes], g_ref[:, lanes]
        w = dot(jnp.concatenate([own_half(x, 0), own_half(x, 1)], axis=0), g, NT)
        for half in range(2):
            r = 2 * q + half
            d1, d2 = decays(run_ref[r : r + 1, :], cols_ref[0][:, r : r + 1], bias)
            first = first + d1 * w[half * TOK : half * TOK + STATE]
            second = second + d2 * w[half * TOK + STATE : half * TOK + TOK, STATE:]

    @pl.when(pl.program_id(0) == 0)
    def _():
        out_ref[...] = jnp.zeros_like(out_ref)

    out_ref[:STATE, :] += first
    out_ref[STATE:, STATE:] += second


def pair_call(x, g, run, cols):
    return pl.pallas_call(
        pair_kernel,
        name="score_gradient",
        grid=(GROUPS,),
        out_shape=jax.ShapeDtypeStruct((TOK, TOK), F32),
        in_specs=[
            pl.BlockSpec((TOK, STEP_FEAT), lambda k: (0, k)),
            pl.BlockSpec((TOK, STEP_FEAT), lambda k: (0, k)),
            pl.BlockSpec((STEP_HEADS, TOK), lambda k: (k, 0)),
            pl.BlockSpec((1, TOK, STEP_HEADS), lambda k: (k, 0, 0)),
        ],
        out_specs=pl.BlockSpec((TOK, TOK), lambda k: (0, 0)),
        compiler_params=pltpu.CompilerParams(vmem_limit_bytes=16 * MIB),
        cost_estimate=pl.CostEstimate(flops=1_500_000_000, bytes_accessed=3_000_000, transcendentals=2_600_000),
    )(x, g, run, cols)


def proj_kernel(tile_ref, pair_ref, proj_ref, high_ref, low_ref, state_ref, grad_ref):
    role = lax.axis_index("seq")
    present = jnp.where(tile_ref[0, 0] == 0, 1.0, 0.0).astype(F32)
    pair = pair_ref[...] * present
    proj = proj_ref[...]
    keys = dot3(pair, proj[:, STATE:], NN)
    query = dot3(pair, proj[:, :STATE], TN)
    both = jnp.concatenate(split2(state_ref[...]), axis=0)
    high = dot(high_ref[...], both, NT)
    across = high[:, :STATE] + high[:, STATE:] + dot(low_ref[...], both[:STATE], NT)
    keys = keys + jnp.where(role == 0, across, 0.0)
    query = query + jnp.where(role == 0, 0.0, across)
    grad_ref[...] = jnp.concatenate([keys, query], axis=1) * (1.0 / SCENES)


def proj_call(tile, pair, proj, high, low, state):
    vm = pl.BlockSpec(memory_space=pltpu.VMEM)
    return pl.pallas_call(
        proj_kernel,
        name="proj_gradient",
        out_shape=jax.ShapeDtypeStruct((TOK, 2 * STATE), F32),
        in_specs=[pl.BlockSpec(memory_space=pltpu.SMEM)] + [vm] * 5,
        out_specs=vm,
        compiler_params=pltpu.CompilerParams(vmem_limit_bytes=16 * MIB),
        cost_estimate=pl.CostEstimate(flops=700_000_000, bytes_accessed=4_000_000, transcendentals=0),
    )(tile, pair, proj, high, low, state)


def ring_place():
    role = lax.axis_index("seq")
    chip = lax.axis_index("dp")
    x, y = chip % 4, chip // 4 % 4
    return jnp.where(role == 0, x, y), jnp.where(role == 0, y, x)


def weight_kernel(grad_ref, other_ref, hidden_ref, wide_ref, *refs):
    outs, sums = refs[:RING], refs[RING]
    role = lax.axis_index("seq")
    own = jnp.concatenate(split2(grad_ref[...]), axis=1)
    other = jnp.concatenate(split2(other_ref[...]), axis=1)
    chunk = 256
    for c in range(HALF // chunk):
        lanes = pl.ds(pl.multiple_of(role * HALF + c * chunk, 128), chunk)
        got = dot(hidden_ref[:, lanes], own, TN)
        got = got + dot(wide_ref[:, c * chunk : (c + 1) * chunk].astype(BF16), other, TN)
        sums[c * chunk : (c + 1) * chunk, :] = got[:, : 2 * STATE] + got[:, 2 * STATE :]
    me, _ = ring_place()
    for k in range(RING):
        to = lax.rem(me + k, RING)
        for b in range(RING):
            place = jnp.where(role == 0, b * RING + to, to * RING + b) * ROWS
            outs[k][b * ROWS : (b + 1) * ROWS, :] = sums[pl.ds(pl.multiple_of(place, 8), ROWS), :]


def weight_call(grad, other, hidden, wide):
    vm = pl.BlockSpec(memory_space=pltpu.VMEM)
    return pl.pallas_call(
        weight_kernel,
        name="weight_gradient",
        out_shape=[jax.ShapeDtypeStruct((PIECE, 2 * STATE), F32)] * RING,
        in_specs=[vm] * 4,
        out_specs=[vm] * RING,
        scratch_shapes=[pltpu.VMEM((HALF, 2 * STATE), F32)],
        compiler_params=pltpu.CompilerParams(vmem_limit_bytes=16 * MIB),
        cost_estimate=pl.CostEstimate(flops=1_400_000_000, bytes_accessed=4_000_000, transcendentals=0),
    )(grad, other, hidden, wide)


def input_kernel(
    tile_ref, x_ref, g_ref, run_ref, cols_ref, scale_ref, step_ref, rates_ref, gain_ref, state_ref, proj_ref,
    dx_ref, dstep_ref, small_ref,
    scores, rows, mine_terms, sums, gains, slopes, direct, owns,
):
    role = lax.axis_index("seq")
    first_role = jnp.where(role == 0, 1.0, 0.0).astype(F32)
    present = jnp.where(tile_ref[0, 0] == 0, 1.0, 0.0).astype(F32)
    k = pl.program_id(0)

    @pl.when(k == 0)
    def _():
        small_ref[...] = jnp.zeros_like(small_ref)
        scores[...] = dot3(proj_ref[:, :STATE], proj_ref[:, STATE:], NT) * present
        gains[...] = jnp.broadcast_to(turn_column(gain_ref[...]), (HEADS, 128))
        mine_high, mine_low = split2(jnp.where(role == 0, proj_ref[:, :STATE], proj_ref[:, STATE:]))
        mine_terms[...] = jnp.concatenate([mine_high, mine_low, mine_high], axis=1)

    bias = causal_bias()
    state_high, state_low = split2(state_ref[...])
    carried = dot(mine_terms[...], jnp.concatenate([state_high, state_high, state_low], axis=0), NN)
    carried = carried * spread_heads(scale_ref[...], STEP_FEAT)
    select = head_rows(STEP_HEADS, STEP_HEADS, STEP_FEAT)
    at = pl.ds(pl.multiple_of(k * STEP_HEADS, STEP_HEADS), STEP_HEADS)
    gain_row = jnp.sum(select * gains[at, :1], axis=0, keepdims=True) * present
    x_all = x_ref[...].astype(F32)
    g_all = g_ref[...].astype(F32)
    own = jnp.where(role == 0, x_all, g_all)
    pick = jnp.concatenate([select, jnp.zeros_like(select)], axis=0).astype(BF16)
    own_high, own_low = split2(own * carried)
    by_own = (dot(pick, own_high, NT) + dot(pick, own_low, NT))[:STEP_HEADS]
    within = []
    for q in range(STEP_HEADS // 2):
        lanes = slice(q * 128, q * 128 + 128)
        x = x_ref[:, lanes]
        upper = jnp.zeros((STATE, 128), F32)
        lower = jnp.zeros((STATE, 128), F32)
        for half in range(2):
            r = 2 * q + half
            g = own_half(g_ref[:, lanes], half)
            d1, d2 = decays(run_ref[r : r + 1, :], cols_ref[0][:, r : r + 1], bias)
            m1 = d1 * scores[:STATE, :]
            m2 = d2 * scores[STATE:, STATE:]
            f1 = m1 * dot(x[:STATE], g, NT)
            f2 = m2 * dot(x[STATE:], g[STATE:], NT)
            sums[:STATE, r : r + 1] = jnp.sum(f1, axis=1, keepdims=True)
            sums[STATE:, r : r + 1] = jnp.sum(f2, axis=1, keepdims=True)
            f1 = jnp.sum(f1, axis=0, keepdims=True)
            f2 = jnp.sum(f2, axis=0, keepdims=True)
            rows[r : r + 1, :STATE] = f1[:, :STATE]
            rows[r : r + 1, STATE:] = f1[:, STATE:] + f2
            h1, l1 = split2(m1)
            h2, l2 = split2(m2)
            upper = upper + dot(h1, g, NN) + dot(l1, g, NN)
            lower = lower + dot(h2, g[STATE:], NN) + dot(l2, g[STATE:], NN)
        within.append(jnp.concatenate([upper, lower], axis=0))
    total = jnp.concatenate(within, axis=1) + first_role * carried
    dx_ref[...] = (total + gain_row * g_all).astype(BF16)

    r8 = lax.broadcasted_iota(jnp.int32, (8, 128), 0)
    lane = lax.broadcasted_iota(jnp.int32, (8, 128), 1)
    gx = jnp.sum(g_all * x_all, axis=0, keepdims=True) * present
    d_gain = jnp.sum(select * gx, axis=1, keepdims=True) * (1.0 / SCENES)
    small_ref[:, 128:] += jnp.where(lane == r8 + k * STEP_HEADS, d_gain, 0.0)
    columns = sums[...].T[:STEP_HEADS]
    direct[at, :] = columns + first_role * by_own
    slopes[at, :] = rows[...] - columns + (1.0 - 2.0 * first_role) * by_own
    owns[at, :] = by_own

    @pl.when(k == GROUPS - 1)
    def _():
        row = lax.broadcasted_iota(jnp.int32, (TOK, TOK), 0)
        col = lax.broadcasted_iota(jnp.int32, (TOK, TOK), 1)
        after = jnp.where(row >= col, 1.0, 0.0).astype(BF16)
        logs = sum_parts(dot(split3(slopes[...]).astype(BF16), after, NN), HEADS)
        logs = logs + first_role * jnp.sum(owns[...], axis=1, keepdims=True)
        step = step_ref[...]
        rate = rates_ref[:, :1]
        dstep_ref[...] = direct[...] / step + rate * logs
        d_rate = rate * present * jnp.sum(step * logs, axis=1, keepdims=True) * (1.0 / SCENES)
        for t in range(GROUPS):
            part = d_rate[t * STEP_HEADS : (t + 1) * STEP_HEADS]
            small_ref[:, :128] += jnp.where(lane == r8 + t * STEP_HEADS, part, 0.0)


def input_call(tile, x, g, run, cols, scale, step, rates, gain, state, proj):
    feat = pl.BlockSpec((TOK, STEP_FEAT), lambda k: (0, k))
    head = pl.BlockSpec((STEP_HEADS, TOK), lambda k: (k, 0))
    return pl.pallas_call(
        input_kernel,
        name="input_gradient",
        grid=(GROUPS,),
        out_shape=(
            jax.ShapeDtypeStruct((TOK, FEAT), BF16),
            jax.ShapeDtypeStruct((HEADS, TOK), F32),
            jax.ShapeDtypeStruct((8, 256), F32),
        ),
        in_specs=[
            pl.BlockSpec(memory_space=pltpu.SMEM),
            feat,
            feat,
            head,
            pl.BlockSpec((1, TOK, STEP_HEADS), lambda k: (k, 0, 0)),
            head,
            pl.BlockSpec((HEADS, TOK), lambda k: (0, 0)),
            pl.BlockSpec((HEADS, 128), lambda k: (0, 0)),
            pl.BlockSpec((1, HEADS), lambda k: (0, 0)),
            pl.BlockSpec((STATE, STEP_FEAT), lambda k: (0, k)),
            pl.BlockSpec((TOK, 2 * STATE), lambda k: (0, 0)),
        ],
        out_specs=(feat, pl.BlockSpec((HEADS, TOK), lambda k: (0, 0)), pl.BlockSpec((8, 256), lambda k: (0, 0))),
        scratch_shapes=[
            pltpu.VMEM((TOK, TOK), F32),
            pltpu.VMEM((STEP_HEADS, TOK), F32),
            pltpu.VMEM((TOK, 3 * STATE), BF16),
            pltpu.VMEM((TOK, 128), F32),
            pltpu.VMEM((HEADS, 128), F32),
            pltpu.VMEM((HEADS, TOK), F32),
            pltpu.VMEM((HEADS, TOK), F32),
            pltpu.VMEM((HEADS, TOK), F32),
        ],
        compiler_params=pltpu.CompilerParams(vmem_limit_bytes=16 * MIB),
        cost_estimate=pl.CostEstimate(flops=6_000_000_000, bytes_accessed=8_000_000, transcendentals=2_600_000),
    )(tile, x, g, run, cols, scale, step, rates, gain, state, proj)


def last_kernel(pieces_ref, out_ref, rate_ref, gain_ref, small, sems):
    role = lax.axis_index("seq")
    few = pltpu.make_async_copy(pieces_ref.at[:, pl.ds(ROWS, 8)], small, sems.at[0])
    few.start()
    rest = pltpu.make_async_copy(pieces_ref.at[:, pl.ds(0, ROWS)], out_ref, sems.at[1])
    rest.start()
    few.wait()
    total = jnp.sum(jnp.sum(small[...], axis=0), axis=0, keepdims=True)
    share = HEADS // 2
    rate_ref[...] = jnp.where(role == 0, total[:, :share], total[:, share:HEADS])
    gain_ref[...] = jnp.where(role == 0, total[:, 128 : 128 + share], total[:, 128 + share : 128 + HEADS])
    rest.wait()


def last_call(pieces):
    hbm = pl.BlockSpec(memory_space=pl.ANY)
    vm = pl.BlockSpec(memory_space=pltpu.VMEM)
    return pl.pallas_call(
        last_kernel,
        name="weight_rows",
        out_shape=(
            jax.ShapeDtypeStruct((PLANE, ROWS, 2 * STATE), F32),
            jax.ShapeDtypeStruct((1, HEADS // 2), F32),
            jax.ShapeDtypeStruct((1, HEADS // 2), F32),
        ),
        in_specs=[hbm],
        out_specs=(hbm, vm, vm),
        scratch_shapes=[pltpu.VMEM((PLANE, 8, 2 * STATE), F32), pltpu.SemaphoreType.DMA((2,))],
        compiler_params=pltpu.CompilerParams(vmem_limit_bytes=16 * MIB),
        cost_estimate=pl.CostEstimate(flops=10_000, bytes_accessed=2_600_000, transcendentals=0),
    )(pieces)


STRIDE = {"z": 16, "y": 4, "x": 1}


def moved(chip, axis, size, new):
    c = chip // STRIDE[axis] % size
    return chip + (new(c) - c) * STRIDE[axis]


def ring_shift(v, stage, k):
    pairs = []
    for core, axes in enumerate(("xy", "yx")):
        for chip in range(SCENES):
            to = moved(chip, axes[stage], RING, lambda c: (c + k) % RING)
            pairs.append((core * SCENES + chip, core * SCENES + to))
    return lax.ppermute(v, ("seq", "dp"), pairs)


def across_z(v, bit):
    return lax.ppermute(v, "dp", [(i, moved(i, "z", 8, lambda c: c ^ bit)) for i in range(SCENES)])


def swap(v):
    return lax.ppermute(v, "seq", [(0, 1), (1, 0)])


def shards(hidden, scan_input, grad_out, step_size, proj_weight, log_rate, skip_gain, tile_list):
    hid, x, g, step = hidden[0], scan_input[0], grad_out[0], step_size[0]
    proj, run, cols, scale, rates, high, low, send, wide = state_call(
        tile_list, hid, proj_weight, x, g, step, log_rate[None]
    )
    state = swap(send)
    wide = swap(wide)
    pair = pair_call(x, g, run, cols)
    grad = proj_call(tile_list, pair, proj, high, low, state)
    pieces = weight_call(grad, swap(grad), hid, wide)
    _, second = ring_place()
    sent = [ring_shift(pieces[k], 0, k) for k in range(1, RING)]
    dx, dstep, small = input_call(tile_list, x, g, run, cols, scale, step, rates, skip_gain[None], state, proj)
    small_own = small
    part = pieces[0] + sent[0] + sent[1] + sent[2]
    part, small_own = lax.optimization_barrier((part, small_own))
    small = small_own + swap(small_own)
    cut = [lax.dynamic_slice_in_dim(part, (second + k) % RING * ROWS, ROWS, 0) for k in range(RING)]
    part = cut[0] + sum(ring_shift(cut[k], 1, k) for k in range(1, RING))
    part = jnp.concatenate([part, small], axis=0)
    for bit in (1, 2, 6):
        part = part + across_z(part, bit)
    plane = [[z * PLANE + i for i in range(PLANE)] for z in range(SCENES // PLANE)]
    pieces = lax.all_to_all(
        jnp.broadcast_to(part, (PLANE,) + part.shape), "dp", 0, 0, axis_index_groups=plane, tiled=True
    )
    grad_weight, d_rate, d_gain = last_call(pieces)
    grad_weight = grad_weight.reshape(HALF, 2 * STATE)
    return dx[None], dstep[None], grad_weight, d_rate[0], d_gain[0]


def solution(mesh):
    in_specs = (
        P("dp", "seq", None),
        P("dp", "seq", None),
        P("dp", "seq", None),
        P("dp", None, "seq"),
        P(),
        P(),
        P(),
        P("dp", "seq"),
    )
    out_specs = (P("dp", "seq", None), P("dp", None, "seq"), P("seq", None), P("seq"), P("seq"))
    return jax.shard_map(shards, mesh=mesh, in_specs=in_specs, out_specs=out_specs, check_vma=False)
```
